128 devices in a mesh: seq: 32 (over y, x, core), head: 4 (over z).
Axes of the slice: x: 4, y: 4, z: 4, core: 2. Of those that a mesh axis runs over, the one named last changes fastest.
Arguments:
- queries: bfloat16 [16384, 8192], P('seq', 'head'), may hold values from -120 to 120
- keys_values: bfloat16 [16384, 2, 1024], P('seq', None, 'head'), may hold values from -6 to 6
- image_kv: bfloat16 [8192, 2, 1024], P('seq', None, 'head'), may hold values from -6 to 6
- image_of: int32 [128], P('seq'), may hold values from 0 to 7
- ancestors: int32 [128, 8], P('seq'), may hold values from 0 to 127, as said below
- counts: int32 [128], P('seq'), may hold values from 0 to 8, as said below
- out_weight: bfloat16 [8192, 4096], P('head'), may hold values from -1.796875 to 1.796875
Outputs:
- projected: bfloat16 [16384, 4096], P('seq', 'head')
The draws below stay inside these ranges and needn't reach their ends.
Inputs may be any that keep to these rules, and one draw needn't show every extreme that they name: `ancestors`: entries at slots a >= counts[b] are 0. A listed entry is a block id; block id g belongs to the aligned group g // 4 of 4 blocks. The blocks listed for the blocks of one aligned group never belong to that group, and no two of them belong to the same group. `counts`: in every draw some block lists the full 8 ancestors.
All inputs are finite; a program needn't handle non-finite values.
Results may differ from the reference program's by a relative error of at most 0.015.
Values may be sent and summed in bfloat16 or wider, within the bound.
A program may use at most 192 MiB of HBM per device.

```python
import jax
import jax.numpy as jnp
from jax import lax

HEADS = 64
KV_HEADS = 8
HEAD_DIM = 128
DOUT = 4096
BS = 128
IMG_TOK = 1024
BLK_DEV = 4
TOKENS = 16384
NBLK = 128
ANC = 8
IMAGES = 8


def shared_keys(key):
    key_base = jax.random.fold_in(key, 101)
    drawn = jax.random.normal(key_base, (TOKENS, KV_HEADS * HEAD_DIM), jnp.float32)
    return jnp.clip(drawn, -6.0, 6.0)


def tree_lists(key):
    shard_total = NBLK // BLK_DEV
    key_pick, key_live, key_order, key_star = jax.random.split(key, 4)
    pick_local = jax.random.randint(key_pick, (shard_total, shard_total), 0, BLK_DEV)
    is_live = jax.random.randint(key_live, (shard_total, shard_total), 0, 5) < 3
    rotation = jax.vmap(lambda one_key: jax.random.permutation(one_key, shard_total))(jax.random.split(key_order, shard_total))
    shard_ids = jnp.arange(shard_total)
    peer_ids = (shard_ids[:, None] + rotation) % shard_total
    self_slot = jnp.argmin(rotation, axis=1)
    block_span = min(BLK_DEV, shard_total)
    forced = (self_slot % BLK_DEV + 1) % block_span
    starred = jax.random.randint(key_star, (), 0, shard_total)
    slot_block = jnp.arange(shard_total) % BLK_DEV
    is_live = is_live | (shard_ids[:, None] == starred) & (slot_block[None, :] == forced[:, None])
    is_live = is_live & (rotation != 0)
    chosen_block = jnp.take_along_axis(pick_local, peer_ids, axis=1)
    global_ids = (peer_ids * BLK_DEV + chosen_block) * is_live.astype(jnp.int32)
    padding_slots = BLK_DEV * ANC - shard_total
    global_ids = jnp.pad(global_ids, ((0, 0), (0, padding_slots)))
    live_flags = jnp.pad(is_live.astype(jnp.int32), ((0, 0), (0, padding_slots)))
    grid_ids = global_ids.reshape(shard_total, ANC, BLK_DEV).transpose(0, 2, 1)
    grid_live = live_flags.reshape(shard_total, ANC, BLK_DEV).transpose(0, 2, 1)
    ranking = jnp.argsort(1 - grid_live, axis=-1, stable=True)
    ancestor_lists = jnp.take_along_axis(grid_ids, ranking, axis=-1)
    totals = jnp.sum(grid_live, axis=-1)
    return (ancestor_lists.reshape(NBLK, ANC).astype(jnp.int32), totals.reshape(NBLK).astype(jnp.int32))


def draw_ancestors(key, part):
    ancestor_lists, totals = tree_lists(key)
    return ancestor_lists


def draw_counts(key, part):
    ancestor_lists, totals = tree_lists(key)
    return totals


def draw_keys_values(key, part):
    keys_part = shared_keys(key)
    key = jax.random.fold_in(key, 7)
    values_part = jnp.clip(jax.random.normal(key, (TOKENS, KV_HEADS * HEAD_DIM), jnp.float32), -6.0, 6.0)
    return jnp.stack([keys_part, values_part], axis=1).astype(jnp.bfloat16)


def draw_queries(key, part):
    key = jax.random.fold_in(key, 9)
    entries = jnp.clip(jax.random.normal(key, (TOKENS, HEADS * HEAD_DIM), jnp.float32), -6.0, 6.0)
    return entries.astype(jnp.bfloat16)


def plant(result, key, low, high):
    place = [jax.random.randint(jax.random.fold_in(key, axis), (), 0, length) for axis, length in enumerate(result.shape)]
    widest = result.shape.index(max(result.shape))
    next_to = place[:widest] + [(place[widest] + 1) % result.shape[widest]] + place[widest + 1:]
    return result.at[tuple(place)].set(low).at[tuple(next_to)].set(high)


def level_of(key, shape, cuts, smallest, top_value):
    loudness, own = 1.0, jax.random.fold_in(key, 6)
    for dim, shards_of in cuts:
        heights = jnp.exp(jax.random.uniform(jax.random.fold_in(own, dim), (shards_of,), jnp.float32, smallest / len(cuts), top_value / len(cuts)))
        loudness = loudness * jnp.repeat(heights, shape[dim] // shards_of).reshape([-1 if axis == dim else 1 for axis in range(len(shape))])
    return loudness


def gaussian(rng, extent, scale, most, shards=(), held_as=jnp.bfloat16):
    loudness = level_of(rng, extent, shards, -0.22, 0.18) if shards else 1.0
    values = jax.random.normal(rng, extent, jnp.float32) * scale * loudness
    return jnp.minimum(jnp.maximum(values, -most), most).astype(held_as)


def setup_inputs(seed: int = 0) -> dict:
    streams_of = jax.random.split(jax.random.key(seed), 8)
    return {
        "queries": draw_queries(jax.random.fold_in(streams_of[7], 71), 0),
        "keys_values": draw_keys_values(jax.random.fold_in(streams_of[7], 71), 0),
        "image_kv": gaussian(streams_of[2], (IMAGES * IMG_TOK, 2, KV_HEADS * HEAD_DIM), 1.0, 6.0, ((0, 32), (2, 4))),
        "image_of": plant(jax.random.randint(streams_of[3], (NBLK,), 0, IMAGES), jax.random.fold_in(streams_of[3], 1), 0, IMAGES - 1).astype(jnp.int32),
        "ancestors": draw_ancestors(jax.random.fold_in(streams_of[7], 71), 0),
        "counts": draw_counts(jax.random.fold_in(streams_of[7], 71), 0),
        "out_weight": gaussian(streams_of[6], (HEADS * HEAD_DIM, DOUT), 0.3, 1.796875, ((0, 4),)),
    }


def attend(query_block, key_rows, value_rows, allowed):
    block_rows = query_block.shape[0]
    kv_heads = key_rows.shape[1] // HEAD_DIM
    grouping = query_block.shape[1] // (kv_heads * HEAD_DIM)
    query_heads = query_block.astype(jnp.float32).reshape(block_rows, kv_heads, grouping, HEAD_DIM)
    key_heads = key_rows.astype(jnp.float32).reshape(-1, kv_heads, HEAD_DIM)
    value_heads = value_rows.astype(jnp.float32).reshape(-1, kv_heads, HEAD_DIM)
    scores = jnp.einsum("rkgd,lkd->kgrl", query_heads, key_heads) * (HEAD_DIM ** -0.5)
    scores = jnp.where(allowed[None, None], scores, -jnp.inf)
    largest = jnp.max(scores, axis=-1, keepdims=True)
    exponent = jnp.exp(scores - largest)
    weights = (exponent / jnp.sum(exponent, axis=-1, keepdims=True)).astype(jnp.bfloat16)
    combined = jnp.einsum("kgrl,lkd->rkgd", weights.astype(jnp.float32), value_heads)
    return combined.astype(jnp.bfloat16).reshape(block_rows, -1)


def allowed_mask(count, slot_count):
    image_part = jnp.ones((BS, IMG_TOK), dtype=bool)
    slot_live = jnp.arange(slot_count, dtype=jnp.int32) < count
    ancestor_part = jnp.broadcast_to(jnp.repeat(slot_live, BS)[None, :], (BS, slot_count * BS))
    positions = jnp.arange(BS, dtype=jnp.int32)
    own_part = positions[None, :] <= positions[:, None]
    return jnp.concatenate([image_part, ancestor_part, own_part], axis=1)


def reference(queries, keys_values, image_kv, image_of, ancestors, counts, out_weight):
    blocks = keys_values.reshape(NBLK, BS, 2, -1)

    def one_block(block_index):
        first_row = (block_index * BS).astype(jnp.int32)
        query_block = lax.dynamic_slice_in_dim(queries, first_row, BS, 0)
        image_start = (image_of[block_index] * IMG_TOK).astype(jnp.int32)
        image_rows = lax.dynamic_slice_in_dim(image_kv, image_start, IMG_TOK, 0)
        ancestor_rows = blocks[ancestors[block_index]].reshape(ANC * BS, 2, -1)
        own_rows = blocks[block_index]
        gathered = jnp.concatenate([image_rows, ancestor_rows, own_rows], axis=0)
        return attend(query_block, gathered[:, 0], gathered[:, 1], allowed_mask(counts[block_index], ANC))

    attended = lax.map(one_block, jnp.arange(NBLK, dtype=jnp.int32)).reshape(TOKENS, -1)
    return jnp.dot(attended, out_weight, preferred_element_type=jnp.float32).astype(jnp.bfloat16)
```

```python
import jax
import jax.numpy as jnp
from jax import lax
from jax.experimental import pallas as pl
from jax.experimental.pallas import tpu as pltpu
from jax.sharding import PartitionSpec as P

HEAD_DIM = 128
BS = 128
IMG_TOK = 1024
ANC = 8
SIDE = 4
BLOCKS = 4
SEQ = 32
KVW = 512
HEADS = 16
GROUP = 4
UNITS = HEADS // GROUP
ROWS = GROUP * BS
KEYS = IMG_TOK + ANC * BS + BS
DSHARE = 1024
HALF = 512
BIG = 1e30
SCALE = HEAD_DIM ** (-0.5)
MESH = pl.DeviceIdType.MESH
A_STEPS = (0, -1, 1, 2)


def kernel(
    image_of, ancestors, counts, q_in, kv_in, im_in, w_in, out_ref,
    kv, im, w, q, s_scr, p_scr, v_scr, att, own, stage, zrecv,
    local_sem, kv_send, kv_recv, im_send, im_recv, z_send, z_recv,
):
    me = lax.axis_index("seq")
    z = lax.axis_index("head")
    core = lax.rem(me, 2)
    x = lax.rem(me // 2, SIDE)
    y = me // (2 * SIDE)

    def chip(da, db, c):
        ox = lax.rem(x + da * (1 - c) + db * c + SIDE, SIDE)
        oy = lax.rem(y + da * c + db * (1 - c) + SIDE, SIDE)
        return (oy * SIDE + ox) * 2 + c

    near = [
        (chip(1, 0, core), z), (chip(-1, 0, core), z), (chip(0, 1, core), z), (chip(0, -1, core), z),
        (me + 1 - 2 * core, z),
        (me, lax.rem(z + 1, SIDE)), (me, lax.rem(z + SIDE - 1, SIDE)),
    ]
    a_up, a_down, b_up, b_down, sibling, z_up, z_down = near

    locals_ = [
        pltpu.make_async_copy(kv_in, kv.at[pl.ds(me * BLOCKS, BLOCKS)], local_sem.at[0]),
        pltpu.make_async_copy(im_in, im.at[pl.ds(me * 2, 2)], local_sem.at[1]),
        pltpu.make_async_copy(q_in, q, local_sem.at[2]),
        pltpu.make_async_copy(w_in, w, local_sem.at[3]),
    ]
    for copy in locals_:
        copy.start()

    barrier = pltpu.get_barrier_semaphore()
    for device in near:
        pl.semaphore_signal(barrier, inc=1, device_id=device, device_id_type=MESH)
    pl.semaphore_wait(barrier, len(near))

    class Gather:
        def __init__(self, buf, source, n, send, recv):
            self.buf, self.source, self.n, self.send, self.recv = buf, source, n, send, recv
            self.started = []
            self.siblings = 0

        def rows(self, da, db, part=None, c=None):
            origin = chip(da, db, core if c is None else c)
            if part is None:
                return self.buf.at[pl.ds(origin * self.n, self.n)]
            half = self.n // 2
            return self.buf.at[pl.ds(origin * self.n + part * half, half)]

        def push(self, src, dst, device, index):
            pltpu.make_async_remote_copy(
                src_ref=src, dst_ref=dst, send_sem=self.send.at[index], recv_sem=self.recv.at[index],
                device_id=device, device_id_type=MESH,
            ).start()
            self.started.append((src, index))

        def arrive(self, ref, index):
            pltpu.make_async_copy(ref, ref, self.recv.at[index]).wait()

        def spread(self, da, src=None):
            ref = self.rows(da, 0)
            src = ref if src is None else src
            i = 4 + A_STEPS.index(da) * 4
            self.push(src, ref, b_up, i)
            self.push(src, ref, b_down, i + 1)

        def pair(self, da, db, src=None):
            ref = self.rows(da, db)
            self.push(ref if src is None else src, ref, sibling, 20 + self.siblings)
            self.siblings += 1

        def begin(self):
            ref = self.rows(0, 0)
            self.push(self.source, ref, a_up, 0)
            self.push(self.source, ref, a_down, 1)
            self.spread(0, self.source)
            self.pair(0, 0, self.source)

        def along_a(self):
            self.arrive(self.rows(-1, 0), 0)
            half = self.rows(-1, 0, 0)
            self.push(half, half, a_up, 2)
            self.spread(-1)
            self.pair(-1, 0)
            self.arrive(self.rows(1, 0), 1)
            half = self.rows(1, 0, 1)
            self.push(half, half, a_down, 3)
            self.spread(1)
            self.pair(1, 0)

        def far_a(self):
            self.arrive(self.rows(2, 0, 0), 2)
            self.arrive(self.rows(2, 0, 1), 3)
            self.spread(2)
            self.pair(2, 0)

        def along_b(self, da):
            i = 4 + A_STEPS.index(da) * 4
            self.arrive(self.rows(da, -1), i)
            half = self.rows(da, -1, 0)
            self.push(half, half, b_up, i + 2)
            self.pair(da, -1)
            self.arrive(self.rows(da, 1), i + 1)
            half = self.rows(da, 1, 1)
            self.push(half, half, b_down, i + 3)
            self.pair(da, 1)

        def far_b(self, da):
            i = 4 + A_STEPS.index(da) * 4
            self.arrive(self.rows(da, 2, 0), i + 2)
            self.arrive(self.rows(da, 2, 1), i + 3)
            self.pair(da, 2)

        def finish(self):
            order = [(0, 0), (-1, 0), (1, 0), (0, -1), (0, 1), (2, 0)]
            for da in A_STEPS[1:]:
                order += [(da, -1), (da, 1)]
            order += [(da, 2) for da in A_STEPS]
            for k, (da, db) in enumerate(order):
                self.arrive(self.rows(da, db, c=1 - core), 20 + k)

        def drain(self):
            for src, index in self.started:
                pltpu.make_async_copy(src, src, self.send.at[index]).wait()

    images = Gather(im, im_in, 2, im_send, im_recv)
    blocks = Gather(kv, kv_in, BLOCKS, kv_send, kv_recv)
    images.begin()
    blocks.begin()
    for g in (images, blocks):
        g.along_a()
        g.along_b(0)
        g.far_a()
        for da in A_STEPS[1:]:
            g.along_b(da)
        for da in A_STEPS:
            g.far_b(da)
    for copy in locals_:
        copy.wait()
    images.finish()
    blocks.finish()

    nt = (((1,), (1,)), ((), ()))
    tt = (((0,), (0,)), ((), ()))

    def dot(a, b, dims):
        return lax.dot_general(a, b, dims, preferred_element_type=jnp.float32)

    def attend(b, u):
        j = u // (UNITS // 2)
        k_lanes = pl.ds(pl.multiple_of(j * HEAD_DIM, HEAD_DIM), HEAD_DIM)
        v_lanes = pl.ds(pl.multiple_of(256 + j * HEAD_DIM, HEAD_DIM), HEAD_DIM)
        q_rows = pl.ds(pl.multiple_of(b * BS, BS), BS)
        heads = [
            pl.ds(pl.multiple_of((u * GROUP + h) * HEAD_DIM, HEAD_DIM), HEAD_DIM) for h in range(GROUP)
        ]
        query = jnp.concatenate([q[q_rows, lanes] for lanes in heads], axis=0)
        image = image_of[b]
        live = jnp.full((1, ROWS), counts[b], jnp.int32)

        def image_step(t, top):
            s = dot(im[image * 8 + t, :, k_lanes], query, nt)
            s_scr[pl.ds(pl.multiple_of(t * BS, BS), BS)] = s
            return jnp.maximum(top, jnp.max(s, axis=0, keepdims=True))

        top = lax.fori_loop(0, IMG_TOK // BS, image_step, jnp.full((1, ROWS), -BIG, jnp.float32))

        def ancestor_step(a, top):
            block = ancestors[b, a]
            s = dot(kv[block, :, k_lanes], query, nt)
            s_scr[pl.ds(pl.multiple_of(IMG_TOK + a * BS, BS), BS)] = s
            v_scr[pl.ds(pl.multiple_of(IMG_TOK + a * BS, BS), BS)] = kv[block, :, v_lanes]
            best = jnp.max(s, axis=0, keepdims=True)
            return jnp.maximum(top, jnp.where(live > a, best, -BIG))

        top = lax.fori_loop(0, ANC, ancestor_step, top)

        block = me * BLOCKS + b
        s = dot(kv[block, :, k_lanes], query, nt)
        key_at = lax.broadcasted_iota(jnp.int32, (BS, ROWS), 0)
        token_at = lax.broadcasted_iota(jnp.int32, (BS, ROWS), 1) & (BS - 1)
        s = jnp.where(key_at <= token_at, s, -BIG)
        s_scr[pl.ds(IMG_TOK + ANC * BS, BS)] = s
        v_scr[pl.ds(IMG_TOK + ANC * BS, BS)] = kv[block, :, v_lanes]
        top = jnp.maximum(top, jnp.max(s, axis=0, keepdims=True))

        def weigh(t, total):
            rows = pl.ds(pl.multiple_of(t * BS, BS), BS)
            slot = t - IMG_TOK // BS
            dead = live <= jnp.where(slot < ANC, slot, -1)
            e = jnp.exp((s_scr[rows] - jnp.where(dead, BIG, top)) * SCALE)
            p_scr[rows] = e.astype(jnp.bfloat16)
            return total + jnp.sum(e, axis=0, keepdims=True)

        total = lax.fori_loop(0, KEYS // BS, weigh, jnp.zeros((1, ROWS), jnp.float32))
        for t in range(IMG_TOK // BS):
            v_scr[pl.ds(t * BS, BS)] = im[image * 8 + t, :, v_lanes]
        o = dot(v_scr[...], p_scr[...], tt)
        o = o / total
        for h, lanes in enumerate(heads):
            att[:, lanes] = o[:, h * BS : (h + 1) * BS].T.astype(jnp.bfloat16)

    def project(d, half):
        cols = pl.ds(pl.multiple_of(d * DSHARE + half * HALF, HALF), HALF)
        return dot(att[...], w[:, cols], (((1,), (0,)), ((), ())))

    far, up, down = lax.rem(z + 2, SIDE), lax.rem(z + 1, SIDE), lax.rem(z + 3, SIDE)

    def z_copy(b, slot, device):
        return pltpu.make_async_remote_copy(
            src_ref=stage.at[b, slot], dst_ref=zrecv.at[b, slot],
            send_sem=z_send.at[b, slot], recv_sem=z_recv.at[b, slot],
            device_id=device, device_id_type=MESH,
        )

    def z_wait(b, slot):
        pltpu.make_async_copy(zrecv.at[b, slot], zrecv.at[b, slot], z_recv.at[b, slot]).wait()

    def one_block(b, carry):
        def unit(u, carry):
            attend(b, u)
            return carry

        lax.fori_loop(0, UNITS, unit, 0)
        for slot, d, half, device in ((0, far, 0, z_up), (1, far, 1, z_down), (2, up, 1, z_up), (3, down, 0, z_down)):
            stage[b, slot] = project(d, half).astype(jnp.bfloat16)
            z_copy(b, slot, device).start()
        for half in range(2):
            own[pl.ds(pl.multiple_of(b * BS, BS), BS), half * HALF : (half + 1) * HALF] = project(z, half)
        for slot, arrived, d, half, device in ((4, 0, up, 0, z_up), (5, 1, down, 1, z_down)):
            part = project(d, half)
            z_wait(b, arrived)
            stage[b, slot] = (part + zrecv[b, arrived].astype(jnp.float32)).astype(jnp.bfloat16)
            z_copy(b, slot, device).start()
        return carry

    lax.fori_loop(0, BLOCKS, one_block, 0)

    def last(b, carry):
        rows = pl.ds(pl.multiple_of(b * BS, BS), BS)
        for slot in (2, 3, 4, 5):
            z_wait(b, slot)
        for half, (one, two) in enumerate(((3, 4), (2, 5))):
            cols = slice(half * HALF, (half + 1) * HALF)
            total = own[rows, cols] + zrecv[b, one].astype(jnp.float32) + zrecv[b, two].astype(jnp.float32)
            out_ref[rows, cols] = total.astype(jnp.bfloat16)
        for slot in range(6):
            pltpu.make_async_copy(stage.at[b, slot], stage.at[b, slot], z_send.at[b, slot]).wait()
        return carry

    lax.fori_loop(0, BLOCKS, last, 0)
    images.drain()
    blocks.drain()


def body(queries, keys_values, image_kv, image_of, ancestors, counts, out_weight):
    kv = keys_values.reshape(BLOCKS, BS, KVW)
    im = image_kv.reshape(2, BS, KVW)
    smem = pl.BlockSpec(memory_space=pltpu.SMEM)
    hbm = pl.BlockSpec(memory_space=pl.ANY)
    bf16, f32 = jnp.bfloat16, jnp.float32
    return pl.pallas_call(
        kernel,
        out_shape=jax.ShapeDtypeStruct((BLOCKS * BS, DSHARE), bf16),
        in_specs=[smem] * 3 + [hbm] * 4,
        out_specs=pl.BlockSpec(memory_space=pltpu.VMEM),
        scratch_shapes=[
            pltpu.VMEM((SEQ * BLOCKS, BS, KVW), bf16),
            pltpu.VMEM((SEQ * 2, BS, KVW), bf16),
            pltpu.VMEM(out_weight.shape, bf16),
            pltpu.VMEM(queries.shape, bf16),
            pltpu.VMEM((KEYS, ROWS), f32),
            pltpu.VMEM((KEYS, ROWS), bf16),
            pltpu.VMEM((KEYS, HEAD_DIM), bf16),
            pltpu.VMEM((BS, HEADS * HEAD_DIM), bf16),
            pltpu.VMEM((BLOCKS * BS, DSHARE), f32),
            pltpu.VMEM((BLOCKS, 6, BS, HALF), bf16),
            pltpu.VMEM((BLOCKS, 6, BS, HALF), bf16),
            pltpu.SemaphoreType.DMA((4,)),
            pltpu.SemaphoreType.DMA((36,)),
            pltpu.SemaphoreType.DMA((36,)),
            pltpu.SemaphoreType.DMA((36,)),
            pltpu.SemaphoreType.DMA((36,)),
            pltpu.SemaphoreType.DMA((BLOCKS, 6)),
            pltpu.SemaphoreType.DMA((BLOCKS, 6)),
        ],
        compiler_params=pltpu.CompilerParams(
            collective_id=0, has_side_effects=True, vmem_limit_bytes=62 * 1024 * 1024
        ),
        name="tree_attention",
    )(image_of, ancestors, counts, queries, kv, im, out_weight)


def solution(mesh):
    in_specs = (
        P("seq", "head"),
        P("seq", None, "head"),
        P("seq", None, "head"),
        P("seq"),
        P("seq", None),
        P("seq"),
        P("head", None),
    )
    out_specs = P("seq", "head")
    return jax.shard_map(body, mesh=mesh, in_specs=in_specs, out_specs=out_specs, check_vma=False)
```

```python
import math

import jax
import jax.numpy as jnp
from jax import lax
from jax.experimental import pallas as pl
from jax.experimental.pallas import tpu as pltpu
from jax.sharding import PartitionSpec as P

HEAD_DIM = 128
BS = 128
IMG_TOK = 1024
ANC = 8
SIDE = 4
BLOCKS = 4
SEQ = 32
KVW = 512
HEADS = 16
GROUP = 4
UNITS = HEADS // GROUP
ROWS = GROUP * BS
DSHARE = 1024
HALF = 512
BIG = 1e30
SCALE2 = HEAD_DIM ** (-0.5) * math.log2(math.e)
MESH = pl.DeviceIdType.MESH
A_STEPS = (0, -1, 1, 2)
HALVES = (2, 3, 6, 7, 10, 11, 14, 15, 18, 19)


def kernel(
    image_of, ancestors, counts, q_in, kv_in, im_in, w_in, out_ref,
    kv, im, w, q, acc, stat, att, own, stage, zrecv,
    local_sem, kv_send, kv_recv, im_send, im_recv, z_send, z_recv,
):
    me = lax.axis_index("seq")
    z = lax.axis_index("head")
    core = lax.rem(me, 2)
    x = lax.rem(me // 2, SIDE)
    y = me // (2 * SIDE)

    def chip(da, db, c):
        ox = lax.rem(x + da * (1 - c) + db * c + SIDE, SIDE)
        oy = lax.rem(y + da * c + db * (1 - c) + SIDE, SIDE)
        return (oy * SIDE + ox) * 2 + c

    near = [
        (chip(1, 0, core), z), (chip(-1, 0, core), z), (chip(0, 1, core), z), (chip(0, -1, core), z),
        (me + 1 - 2 * core, z),
        (me, lax.rem(z + 1, SIDE)), (me, lax.rem(z + SIDE - 1, SIDE)),
    ]
    a_up, a_down, b_up, b_down, sibling, z_up, z_down = near

    locals_ = [
        pltpu.make_async_copy(kv_in, kv.at[pl.ds(me * BLOCKS, BLOCKS)], local_sem.at[0]),
        pltpu.make_async_copy(im_in, im.at[pl.ds(me * 2, 2)], local_sem.at[1]),
        pltpu.make_async_copy(q_in, q, local_sem.at[2]),
        pltpu.make_async_copy(w_in, w, local_sem.at[3]),
    ]
    for copy in locals_:
        copy.start()

    barrier = pltpu.get_barrier_semaphore()
    for device in near:
        pl.semaphore_signal(barrier, inc=1, device_id=device, device_id_type=MESH)
    pl.semaphore_wait(barrier, len(near))

    class Gather:
        def __init__(self, buf, source, n, send, recv):
            self.buf, self.source, self.n, self.send, self.recv = buf, source, n, send, recv
            self.started = []
            self.siblings = 0

        def rows(self, da, db, part=None, c=None):
            origin = chip(da, db, core if c is None else c)
            if part is None:
                return self.buf.at[pl.ds(origin * self.n, self.n)]
            half = self.n // 2
            return self.buf.at[pl.ds(origin * self.n + part * half, half)]

        def push(self, src, dst, device, index):
            pltpu.make_async_remote_copy(
                src_ref=src, dst_ref=dst, send_sem=self.send.at[index], recv_sem=self.recv.at[index],
                device_id=device, device_id_type=MESH,
            ).start()
            self.started.append(index)

        def arrive(self, ref, index):
            pltpu.make_async_copy(ref, ref, self.recv.at[index]).wait()

        def spread(self, da, src=None):
            ref = self.rows(da, 0)
            src = ref if src is None else src
            i = 4 + A_STEPS.index(da) * 4
            self.push(src, ref, b_up, i)
            self.push(src, ref, b_down, i + 1)

        def pair(self, da, db, src=None):
            ref = self.rows(da, db)
            self.push(ref if src is None else src, ref, sibling, 20 + self.siblings)
            self.siblings += 1

        def begin(self):
            ref = self.rows(0, 0)
            self.push(self.source, ref, a_up, 0)
            self.push(self.source, ref, a_down, 1)
            self.spread(0, self.source)
            self.pair(0, 0, self.source)

        def along_a(self):
            self.arrive(self.rows(-1, 0), 0)
            half = self.rows(-1, 0, 0)
            self.push(half, half, a_up, 2)
            self.spread(-1)
            self.pair(-1, 0)
            self.arrive(self.rows(1, 0), 1)
            half = self.rows(1, 0, 1)
            self.push(half, half, a_down, 3)
            self.spread(1)
            self.pair(1, 0)

        def far_a(self):
            self.arrive(self.rows(2, 0, 0), 2)
            self.arrive(self.rows(2, 0, 1), 3)
            self.spread(2)
            self.pair(2, 0)

        def along_b(self, da):
            i = 4 + A_STEPS.index(da) * 4
            self.arrive(self.rows(da, -1), i)
            half = self.rows(da, -1, 0)
            self.push(half, half, b_up, i + 2)
            self.pair(da, -1)
            self.arrive(self.rows(da, 1), i + 1)
            half = self.rows(da, 1, 1)
            self.push(half, half, b_down, i + 3)
            self.pair(da, 1)

        def far_b(self, da):
            i = 4 + A_STEPS.index(da) * 4
            self.arrive(self.rows(da, 2, 0), i + 2)
            self.arrive(self.rows(da, 2, 1), i + 3)
            self.pair(da, 2)

        def finish(self):
            order = [(0, 0), (-1, 0), (1, 0), (0, -1), (0, 1), (2, 0)]
            for da in A_STEPS[1:]:
                order += [(da, -1), (da, 1)]
            order += [(da, 2) for da in A_STEPS]
            for k, (da, db) in enumerate(order):
                self.arrive(self.rows(da, db, c=1 - core), 20 + k)

        def drain(self):
            for index in self.started:
                part = self.n // 2 if index in HALVES else self.n
                ref = self.buf.at[pl.ds(0, part)]
                pltpu.make_async_copy(ref, ref, self.send.at[index]).wait()

    images = Gather(im, im_in, 2, im_send, im_recv)
    blocks = Gather(kv, kv_in, BLOCKS, kv_send, kv_recv)
    images.begin()
    images.along_a()
    blocks.begin()
    images.along_b(0)
    images.far_a()
    for da in A_STEPS[1:]:
        images.along_b(da)
    for da in A_STEPS:
        images.far_b(da)
    for copy in locals_[:3]:
        copy.wait()
    images.finish()

    nt = (((1,), (1,)), ((), ()))
    nn = (((1,), (0,)), ((), ()))

    def dot(a, b, dims):
        return lax.dot_general(a, b, dims, preferred_element_type=jnp.float32)

    def queries_of(b, u):
        rows = pl.ds(pl.multiple_of(b * BS, BS), BS)
        lanes = [
            pl.ds(pl.multiple_of((u * GROUP + h) * HEAD_DIM, HEAD_DIM), HEAD_DIM) for h in range(GROUP)
        ]
        return jnp.concatenate([q[rows, cols] for cols in lanes], axis=0)

    def lanes_of(j):
        return (
            pl.ds(pl.multiple_of(j * HEAD_DIM, HEAD_DIM), HEAD_DIM),
            pl.ds(pl.multiple_of(256 + j * HEAD_DIM, HEAD_DIM), HEAD_DIM),
        )

    def image_part(b, j):
        k_lanes, v_lanes = lanes_of(j)
        image = image_of[b]
        tiles = range(IMG_TOK // BS)
        k = jnp.concatenate([im[image * 8 + t, :, k_lanes] for t in tiles], axis=0)
        v = jnp.concatenate([im[image * 8 + t, :, v_lanes] for t in tiles], axis=0).T
        for r in range(2):
            u = 2 * j + r
            s = dot(k, queries_of(b, u), nt)
            top = jnp.max(s, axis=0, keepdims=True)
            e = jnp.exp2((s - top) * SCALE2)
            slot = b * UNITS + u
            stat[slot, 0:1] = top
            stat[slot, 1:2] = jnp.sum(e, axis=0, keepdims=True)
            acc[slot] = dot(v, e.astype(jnp.bfloat16), nn)

    def rest_part(b, j):
        k_lanes, v_lanes = lanes_of(j)
        live = jnp.full((1, ROWS), counts[b], jnp.int32)
        at = [ancestors[b, a] for a in range(ANC)] + [me * BLOCKS + b]
        k = jnp.concatenate([kv[i, :, k_lanes] for i in at], axis=0)
        v = jnp.concatenate([kv[i, :, v_lanes] for i in at], axis=0).T
        key_at = lax.broadcasted_iota(jnp.int32, (BS, ROWS), 0)
        token_at = lax.broadcasted_iota(jnp.int32, (BS, ROWS), 1) & (BS - 1)
        for r in range(2):
            u = 2 * j + r
            slot = b * UNITS + u
            s = dot(k, queries_of(b, u), nt)
            parts = [s[a * BS : (a + 1) * BS] for a in range(ANC + 1)]
            parts[ANC] = jnp.where(key_at <= token_at, parts[ANC], -BIG)
            before = stat[slot, 0:1]
            top = jnp.maximum(before, jnp.max(parts[ANC], axis=0, keepdims=True))
            for a in range(ANC):
                best = jnp.max(parts[a], axis=0, keepdims=True)
                top = jnp.maximum(top, jnp.where(live > a, best, -BIG))
            keep = jnp.exp2((before - top) * SCALE2)
            total = stat[slot, 1:2] * keep
            weights = []
            for a in range(ANC + 1):
                under = jnp.where(live > a, top, BIG) if a < ANC else top
                e = jnp.exp2((parts[a] - under) * SCALE2)
                total = total + jnp.sum(e, axis=0, keepdims=True)
                weights.append(e.astype(jnp.bfloat16))
            o = acc[slot] * keep + dot(v, jnp.concatenate(weights, axis=0), nn)
            o = o / total
            for h in range(GROUP):
                cols = pl.ds(pl.multiple_of((u * GROUP + h) * HEAD_DIM, HEAD_DIM), HEAD_DIM)
                att[:, cols] = o[:, h * BS : (h + 1) * BS].T.astype(jnp.bfloat16)

    def project(d, half):
        cols = pl.ds(pl.multiple_of(d * DSHARE + half * HALF, HALF), HALF)
        return dot(att[...], w[:, cols], nn)

    far, up, down = lax.rem(z + 2, SIDE), lax.rem(z + 1, SIDE), lax.rem(z + 3, SIDE)

    def z_copy(b, slot, device):
        return pltpu.make_async_remote_copy(
            src_ref=stage.at[b, slot], dst_ref=zrecv.at[b, slot],
            send_sem=z_send.at[b, slot], recv_sem=z_recv.at[b, slot],
            device_id=device, device_id_type=MESH,
        )

    def z_wait(b, slot):
        pltpu.make_async_copy(zrecv.at[b, slot], zrecv.at[b, slot], z_recv.at[b, slot]).wait()

    def one_block(b, carry):
        def heads(j, carry):
            rest_part(b, j)
            return carry

        lax.fori_loop(0, 2, heads, 0)
        for slot, d, half, device in ((0, far, 0, z_up), (1, far, 1, z_down), (2, up, 1, z_up), (3, down, 0, z_down)):
            stage[b, slot] = project(d, half).astype(jnp.bfloat16)
            z_copy(b, slot, device).start()
        for half in range(2):
            own[pl.ds(pl.multiple_of(b * BS, BS), BS), half * HALF : (half + 1) * HALF] = project(z, half)
        for slot, arrived, d, half, device in ((4, 0, up, 0, z_up), (5, 1, down, 1, z_down)):
            part = project(d, half)
            z_wait(b, arrived)
            stage[b, slot] = (part + zrecv[b, arrived].astype(jnp.float32)).astype(jnp.bfloat16)
            z_copy(b, slot, device).start()
        return carry

    events = [
        blocks.along_a, lambda: blocks.along_b(0), blocks.far_a,
        lambda: blocks.along_b(-1), lambda: blocks.along_b(1), lambda: blocks.along_b(2),
    ]

    def image_step(i, carry):
        for k, event in enumerate(events):
            pl.when(i == k)(event)
        image_part(i // 2, lax.rem(i, 2))
        return carry

    lax.fori_loop(0, 2 * BLOCKS, image_step, 0)
    for da in A_STEPS:
        blocks.far_b(da)
    locals_[3].wait()
    blocks.finish()
    lax.fori_loop(0, BLOCKS, one_block, 0)

    def last(b, carry):
        rows = pl.ds(pl.multiple_of(b * BS, BS), BS)
        for slot in (2, 3, 4, 5):
            z_wait(b, slot)
        for half, (one, two) in enumerate(((3, 4), (2, 5))):
            cols = slice(half * HALF, (half + 1) * HALF)
            total = own[rows, cols] + zrecv[b, one].astype(jnp.float32) + zrecv[b, two].astype(jnp.float32)
            out_ref[rows, cols] = total.astype(jnp.bfloat16)
        for slot in range(6):
            pltpu.make_async_copy(stage.at[b, slot], stage.at[b, slot], z_send.at[b, slot]).wait()
        return carry

    lax.fori_loop(0, BLOCKS, last, 0)
    images.drain()
    blocks.drain()


def body(queries, keys_values, image_kv, image_of, ancestors, counts, out_weight):
    kv = keys_values.reshape(BLOCKS, BS, KVW)
    im = image_kv.reshape(2, BS, KVW)
    smem = pl.BlockSpec(memory_space=pltpu.SMEM)
    hbm = pl.BlockSpec(memory_space=pl.ANY)
    bf16, f32 = jnp.bfloat16, jnp.float32
    return pl.pallas_call(
        kernel,
        out_shape=jax.ShapeDtypeStruct((BLOCKS * BS, DSHARE), bf16),
        in_specs=[smem] * 3 + [hbm] * 4,
        out_specs=pl.BlockSpec(memory_space=pltpu.VMEM),
        scratch_shapes=[
            pltpu.VMEM((SEQ * BLOCKS, BS, KVW), bf16),
            pltpu.VMEM((SEQ * 2, BS, KVW), bf16),
            pltpu.VMEM(out_weight.shape, bf16),
            pltpu.VMEM(queries.shape, bf16),
            pltpu.VMEM((BLOCKS * UNITS, HEAD_DIM, ROWS), f32),
            pltpu.VMEM((BLOCKS * UNITS, 8, ROWS), f32),
            pltpu.VMEM((BS, HEADS * HEAD_DIM), bf16),
            pltpu.VMEM((BLOCKS * BS, DSHARE), f32),
            pltpu.VMEM((BLOCKS, 6, BS, HALF), bf16),
            pltpu.VMEM((BLOCKS, 6, BS, HALF), bf16),
            pltpu.SemaphoreType.DMA((4,)),
            pltpu.SemaphoreType.DMA((36,)),
            pltpu.SemaphoreType.DMA((36,)),
            pltpu.SemaphoreType.DMA((36,)),
            pltpu.SemaphoreType.DMA((36,)),
            pltpu.SemaphoreType.DMA((BLOCKS, 6)),
            pltpu.SemaphoreType.DMA((BLOCKS, 6)),
        ],
        compiler_params=pltpu.CompilerParams(
            collective_id=0, has_side_effects=True, vmem_limit_bytes=62 * 1024 * 1024
        ),
        name="tree_attention",
    )(image_of, ancestors, counts, queries, kv, im, out_weight)


def solution(mesh):
    in_specs = (
        P("seq", "head"),
        P("seq", None, "head"),
        P("seq", None, "head"),
        P("seq"),
        P("seq", None),
        P("seq"),
        P("head", None),
    )
    out_specs = P("seq", "head")
    return jax.shard_map(body, mesh=mesh, in_specs=in_specs, out_specs=out_specs, check_vma=False)
```

```python
import math

import jax
import jax.numpy as jnp
from jax import lax
from jax.experimental import pallas as pl
from jax.experimental.pallas import tpu as pltpu
from jax.sharding import PartitionSpec as P

HEAD_DIM = 128
BS = 128
IMG_TOK = 1024
ANC = 8
SIDE = 4
BLOCKS = 4
SEQ = 32
KVW = 512
HEADS = 16
GROUP = 4
UNITS = HEADS // GROUP
ROWS = GROUP * BS
DSHARE = 1024
HALF = 512
BIG = 1e30
SCALE2 = HEAD_DIM ** (-0.5) * math.log2(math.e)
MESH = pl.DeviceIdType.MESH
A_STEPS = (0, -1, 1, 2)
HALVES = (2, 3, 6, 7, 10, 11, 14, 15, 18, 19)


def kernel(
    image_of, ancestors, counts, q_in, kv_in, im_in, w_in, out_ref,
    im, w, q, acc, stat, att, hold, own, stage, zrecv,
    row_own, row_prev, row_next, row_far, picked, passing, got, table, needs,
    local_sem, im_send, im_recv, row_send, row_recv, pass_send, pass_recv, got_send, got_recv,
    table_send, table_recv, z_send, z_recv,
):
    me = lax.axis_index("seq")
    z = lax.axis_index("head")
    core = lax.rem(me, 2)
    x = lax.rem(me // 2, SIDE)
    y = me // (2 * SIDE)

    def chip(da, db, c):
        ox = lax.rem(x + da * (1 - c) + db * c + SIDE, SIDE)
        oy = lax.rem(y + da * c + db * (1 - c) + SIDE, SIDE)
        return (oy * SIDE + ox) * 2 + c

    def other(device):
        return device + 1 - 2 * core

    a_up, a_down = (chip(1, 0, core), z), (chip(-1, 0, core), z)
    b_up, b_down = (chip(0, 1, core), z), (chip(0, -1, core), z)
    sibling = (other(me), z)
    z_up, z_down = (me, lax.rem(z + 1, SIDE)), (me, lax.rem(z + SIDE - 1, SIDE))
    near = [sibling, z_up, z_down]
    for da, db in ((1, 0), (-1, 0), (2, 0), (0, 1), (0, -1), (0, 2)):
        near += [(chip(da, db, 0), z), (chip(da, db, 1), z)]

    locals_ = [
        pltpu.make_async_copy(kv_in, row_own, local_sem.at[0]),
        pltpu.make_async_copy(im_in, im.at[pl.ds(me * 2, 2)], local_sem.at[1]),
        pltpu.make_async_copy(q_in, q, local_sem.at[2]),
        pltpu.make_async_copy(w_in, w, local_sem.at[3]),
    ]
    for copy in locals_:
        copy.start()

    barrier = pltpu.get_barrier_semaphore()
    for device in near:
        pl.semaphore_signal(barrier, inc=1, device_id=device, device_id_type=MESH)

    lane = lax.broadcasted_iota(jnp.int32, (8, 128), 1)
    listed = jnp.zeros((8, 128), jnp.int32)
    for b in range(BLOCKS):
        for a in range(ANC):
            block = jnp.full((8, 128), ancestors[b, a], jnp.int32)
            listed = jnp.maximum(listed, jnp.where((block >> 2) == lane, block & 3, 0))
    table[0, 0] = listed

    pl.semaphore_wait(barrier, len(near))

    def copy_to(src, dst, send, recv, device):
        return pltpu.make_async_remote_copy(
            src_ref=src, dst_ref=dst, send_sem=send, recv_sem=recv, device_id=device, device_id_type=MESH,
        )

    def wait_for(ref, sem):
        pltpu.make_async_copy(ref, ref, sem).wait()

    table_slots = [(k, r) for k in range(SIDE) for r in range(2) if (k, r) != (0, 0)]
    for k, r in table_slots:
        device = (chip(0, -k, core if r == 0 else 1 - core), z)
        copy_to(table.at[0, 0], table.at[k, r], table_send.at[k, r], table_recv.at[k, r], device).start()

    class Gather:
        def __init__(self, buf, source, n, send, recv):
            self.buf, self.source, self.n, self.send, self.recv = buf, source, n, send, recv
            self.started = []
            self.siblings = 0

        def rows(self, da, db, part=None, c=None):
            origin = chip(da, db, core if c is None else c)
            if part is None:
                return self.buf.at[pl.ds(origin * self.n, self.n)]
            half = self.n // 2
            return self.buf.at[pl.ds(origin * self.n + part * half, half)]

        def push(self, src, dst, device, index):
            pltpu.make_async_remote_copy(
                src_ref=src, dst_ref=dst, send_sem=self.send.at[index], recv_sem=self.recv.at[index],
                device_id=device, device_id_type=MESH,
            ).start()
            self.started.append(index)

        def arrive(self, ref, index):
            pltpu.make_async_copy(ref, ref, self.recv.at[index]).wait()

        def spread(self, da, src=None):
            ref = self.rows(da, 0)
            src = ref if src is None else src
            i = 4 + A_STEPS.index(da) * 4
            self.push(src, ref, b_up, i)
            self.push(src, ref, b_down, i + 1)

        def pair(self, da, db, src=None):
            ref = self.rows(da, db)
            self.push(ref if src is None else src, ref, sibling, 20 + self.siblings)
            self.siblings += 1

        def begin(self):
            ref = self.rows(0, 0)
            self.push(self.source, ref, a_up, 0)
            self.push(self.source, ref, a_down, 1)
            self.spread(0, self.source)
            self.pair(0, 0, self.source)

        def along_a(self):
            self.arrive(self.rows(-1, 0), 0)
            half = self.rows(-1, 0, 0)
            self.push(half, half, a_up, 2)
            self.spread(-1)
            self.pair(-1, 0)
            self.arrive(self.rows(1, 0), 1)
            half = self.rows(1, 0, 1)
            self.push(half, half, a_down, 3)
            self.spread(1)
            self.pair(1, 0)

        def far_a(self):
            self.arrive(self.rows(2, 0, 0), 2)
            self.arrive(self.rows(2, 0, 1), 3)
            self.spread(2)
            self.pair(2, 0)

        def along_b(self, da):
            i = 4 + A_STEPS.index(da) * 4
            self.arrive(self.rows(da, -1), i)
            half = self.rows(da, -1, 0)
            self.push(half, half, b_up, i + 2)
            self.pair(da, -1)
            self.arrive(self.rows(da, 1), i + 1)
            half = self.rows(da, 1, 1)
            self.push(half, half, b_down, i + 3)
            self.pair(da, 1)

        def far_b(self, da):
            i = 4 + A_STEPS.index(da) * 4
            self.arrive(self.rows(da, 2, 0), i + 2)
            self.arrive(self.rows(da, 2, 1), i + 3)
            self.pair(da, 2)

        def finish(self):
            order = [(0, 0), (-1, 0), (1, 0), (0, -1), (0, 1), (2, 0)]
            for da in A_STEPS[1:]:
                order += [(da, -1), (da, 1)]
            order += [(da, 2) for da in A_STEPS]
            for k, (da, db) in enumerate(order):
                self.arrive(self.rows(da, db, c=1 - core), 20 + k)

        def drain(self):
            for index in self.started:
                part = self.n // 2 if index in HALVES else self.n
                ref = self.buf.at[pl.ds(0, part)]
                pltpu.make_async_copy(ref, ref, self.send.at[index]).wait()

    images = Gather(im, im_in, 2, im_send, im_recv)
    low, high = pl.ds(0, 2), pl.ds(2, 2)
    row_copies = [
        copy_to(kv_in.at[low], row_prev.at[low], row_send.at[0], row_recv.at[0], a_up),
        copy_to(kv_in.at[high], row_next.at[high], row_send.at[1], row_recv.at[1], a_down),
        copy_to(kv_in.at[high], row_prev.at[high], row_send.at[2], row_recv.at[2], a_up),
        copy_to(kv_in.at[low], row_next.at[low], row_send.at[3], row_recv.at[3], a_down),
        copy_to(row_prev.at[low], row_far.at[low], row_send.at[4], row_recv.at[4], a_up),
        copy_to(row_next.at[high], row_far.at[high], row_send.at[5], row_recv.at[5], a_down),
    ]

    def row_begin():
        for copy in row_copies[:4]:
            copy.start()

    def row_pass():
        row_copies[0].wait_recv()
        row_copies[4].start()
        row_copies[1].wait_recv()
        row_copies[5].start()

    SIDES = (0, -1, 1, 2)

    def origin(r, k, i):
        return chip(A_STEPS[i], SIDES[k], core if r == 0 else 1 - core)

    def deliver(src, r, k, i, source, device):
        if r == 1:
            device = (other(device[0]), z)
        return copy_to(src, got.at[source], got_send.at[r, k, i], got_recv.at[r, k, i], device)

    def pass_copy(r, i):
        device = b_up if i < 2 else b_down
        return copy_to(picked.at[2, r, i], passing.at[r, i], pass_send.at[r, i], pass_recv.at[r, i], device)

    def hand_on(r, i):
        device, back = (b_up, -1) if i < 2 else (b_down, 1)
        return deliver(passing.at[r, i], r, 3, i, chip(A_STEPS[i], back, core), device)

    def pick(i, row):
        source = chip(A_STEPS[i], 0, core)
        for r in range(2):
            picked[2, r, i] = row[needs[2, r, 0, source]]
            pass_copy(r, i).start()
        for n, (k, slot, device) in enumerate(((1, 1, b_up), (2, 3, b_down))):
            for r in range(2):
                picked[n, r, i] = row[needs[slot, r, 0, source]]
                deliver(picked.at[n, r, i], r, k, i, source, device).start()
        picked[3, 1, i] = row[needs[0, 1, 0, source]]
        deliver(picked.at[3, 1, i], 1, 0, i, source, (me, z)).start()
        got[source] = row[needs[0, 0, 0, source]]

    images.begin()
    row_begin()
    images.along_a()
    for k, r in table_slots:
        wait_for(table.at[k, r], table_recv.at[k, r])
    to_scalars = pltpu.make_async_copy(table, needs, local_sem.at[4])
    to_scalars.start()
    images.along_b(0)
    images.far_a()
    to_scalars.wait()
    locals_[0].wait()
    pick(0, row_own)
    row_pass()
    for da in A_STEPS[1:]:
        images.along_b(da)
    row_copies[2].wait_recv()
    pick(1, row_prev)
    row_copies[3].wait_recv()
    pick(2, row_next)
    for da in A_STEPS:
        images.far_b(da)
    row_copies[4].wait_recv()
    row_copies[5].wait_recv()
    pick(3, row_far)
    for copy in locals_[1:3]:
        copy.wait()
    images.finish()

    nt = (((1,), (1,)), ((), ()))
    nn = (((1,), (0,)), ((), ()))

    def dot(a, b, dims):
        return lax.dot_general(a, b, dims, preferred_element_type=jnp.float32)

    def queries_of(b, u):
        rows = pl.ds(pl.multiple_of(b * BS, BS), BS)
        lanes = [
            pl.ds(pl.multiple_of((u * GROUP + h) * HEAD_DIM, HEAD_DIM), HEAD_DIM) for h in range(GROUP)
        ]
        return jnp.concatenate([q[rows, cols] for cols in lanes], axis=0)

    def lanes_of(j):
        return (
            pl.ds(pl.multiple_of(j * HEAD_DIM, HEAD_DIM), HEAD_DIM),
            pl.ds(pl.multiple_of(256 + j * HEAD_DIM, HEAD_DIM), HEAD_DIM),
        )

    key_at = lax.broadcasted_iota(jnp.int32, (BS, ROWS), 0)
    token_at = lax.broadcasted_iota(jnp.int32, (BS, ROWS), 1) & (BS - 1)

    def image_part(b, j):
        lanes = lanes_of(j)
        image = image_of[b]
        k, v = (
            jnp.concatenate(
                [im[image * 8 + t, :, cols] for t in range(IMG_TOK // BS)] + [row_own[b, :, cols]], axis=0
            )
            for cols in lanes
        )
        v = v.T
        for r in range(2):
            u = 2 * j + r
            slot = b * UNITS + u
            s = dot(k, queries_of(b, u), nt)
            s, s_own = s[:IMG_TOK], s[IMG_TOK:]
            s_own = jnp.where(key_at <= token_at, s_own, -BIG)
            top = jnp.maximum(jnp.max(s, axis=0, keepdims=True), jnp.max(s_own, axis=0, keepdims=True))
            e = jnp.exp2((s - top) * SCALE2)
            e_own = jnp.exp2((s_own - top) * SCALE2)
            stat[slot, 0:1] = top
            stat[slot, 1:2] = jnp.sum(e, axis=0, keepdims=True) + jnp.sum(e_own, axis=0, keepdims=True)
            acc[slot] = dot(v, jnp.concatenate([e.astype(jnp.bfloat16), e_own.astype(jnp.bfloat16)], axis=0), nn)

    def rest_part(b, j):
        k_lanes, v_lanes = lanes_of(j)
        live = jnp.full((1, ROWS), counts[b], jnp.int32)
        at = [lax.shift_right_logical(ancestors[b, a], 2) for a in range(ANC)]
        k = jnp.concatenate([got[i, :, k_lanes] for i in at], axis=0)
        v = jnp.concatenate([got[i, :, v_lanes] for i in at], axis=0).T
        for r in range(2):
            u = 2 * j + r
            slot = b * UNITS + u
            s = dot(k, queries_of(b, u), nt)
            parts = [s[a * BS : (a + 1) * BS] for a in range(ANC)]
            before = stat[slot, 0:1]
            top = before
            for a in range(ANC):
                best = jnp.max(parts[a], axis=0, keepdims=True)
                top = jnp.maximum(top, jnp.where(live > a, best, -BIG))
            keep = jnp.exp2((before - top) * SCALE2)
            total = stat[slot, 1:2] * keep
            weights = []
            for a in range(ANC):
                under = jnp.where(live > a, top, BIG)
                e = jnp.exp2((parts[a] - under) * SCALE2)
                total = total + jnp.sum(e, axis=0, keepdims=True)
                weights.append(e.astype(jnp.bfloat16))
            o = acc[slot] * keep + dot(v, jnp.concatenate(weights, axis=0), nn)
            o = o / total
            for h in range(GROUP):
                cols = pl.ds(pl.multiple_of((u * GROUP + h) * HEAD_DIM, HEAD_DIM), HEAD_DIM)
                att[:, cols] = o[:, h * BS : (h + 1) * BS].T.astype(jnp.bfloat16)

    def project(d, half):
        cols = pl.ds(pl.multiple_of(d * DSHARE + half * HALF, HALF), HALF)
        return dot(att[...], w[:, cols], nn)

    far, up, down = lax.rem(z + 2, SIDE), lax.rem(z + 1, SIDE), lax.rem(z + 3, SIDE)

    def z_copy(b, slot, device):
        return pltpu.make_async_remote_copy(
            src_ref=stage.at[b, slot], dst_ref=zrecv.at[b, slot],
            send_sem=z_send.at[b, slot], recv_sem=z_recv.at[b, slot],
            device_id=device, device_id_type=MESH,
        )

    def z_wait(b, slot):
        wait_for(zrecv.at[b, slot], z_recv.at[b, slot])

    def pass_on(b):
        for k, (slot, device) in enumerate(((4, z_up), (5, z_down))):
            z_wait(b, k)
            stage[b, slot] = (hold[k] + zrecv[b, k].astype(jnp.float32)).astype(jnp.bfloat16)
            z_copy(b, slot, device).start()

    def one_block(b, carry):
        def heads(j, carry):
            rest_part(b, j)
            return carry

        lax.fori_loop(0, 2, heads, 0)

        def send_partial(slot, d, half, device):
            stage[b, slot] = project(d, half).astype(jnp.bfloat16)
            z_copy(b, slot, device).start()

        send_partial(0, far, 0, z_up)
        send_partial(1, far, 1, z_down)
        pl.when(b > 0)(lambda: pass_on(b - 1))
        send_partial(2, up, 1, z_up)
        send_partial(3, down, 0, z_down)
        hold[0] = project(up, 0)
        hold[1] = project(down, 1)
        for half in range(2):
            own[pl.ds(pl.multiple_of(b * BS, BS), BS), half * HALF : (half + 1) * HALF] = project(z, half)
        return carry

    def forward(i):
        for r in range(2):
            pass_copy(r, i).wait_recv()
            hand_on(r, i).start()

    def image_step(i, carry):
        for k, n in enumerate((0, 2, 1, 3)):
            pl.when(i == 2 * k)(lambda n=n: forward(n))
        image_part(i // 2, lax.rem(i, 2))
        return carry

    lax.fori_loop(0, 2 * BLOCKS, image_step, 0)
    arrivals = [(r, k, i) for r in range(2) for k in range(4) for i in range(4) if (r, k) != (0, 0)]
    for r, k, i in arrivals:
        wait_for(got.at[origin(r, k, i)], got_recv.at[r, k, i])
    locals_[3].wait()
    lax.fori_loop(0, BLOCKS, one_block, 0)
    pass_on(BLOCKS - 1)

    def last(b, carry):
        rows = pl.ds(pl.multiple_of(b * BS, BS), BS)
        for slot in (2, 3, 4, 5):
            z_wait(b, slot)
        for half, (one, two) in enumerate(((3, 4), (2, 5))):
            cols = slice(half * HALF, (half + 1) * HALF)
            total = own[rows, cols] + zrecv[b, one].astype(jnp.float32) + zrecv[b, two].astype(jnp.float32)
            out_ref[rows, cols] = total.astype(jnp.bfloat16)
        for slot in range(6):
            wait_for(stage.at[b, slot], z_send.at[b, slot])
        return carry

    lax.fori_loop(0, BLOCKS, last, 0)
    images.drain()
    for k, r in table_slots:
        wait_for(table.at[0, 0], table_send.at[k, r])
    for copy in row_copies:
        copy.wait_send()
    for r in range(2):
        for i in range(4):
            pass_copy(r, i).wait_send()
    for r, k, i in arrivals:
        wait_for(got.at[0], got_send.at[r, k, i])


def body(queries, keys_values, image_kv, image_of, ancestors, counts, out_weight):
    kv = keys_values.reshape(BLOCKS, BS, KVW)
    im = image_kv.reshape(2, BS, KVW)
    smem = pl.BlockSpec(memory_space=pltpu.SMEM)
    hbm = pl.BlockSpec(memory_space=pl.ANY)
    bf16, f32 = jnp.bfloat16, jnp.float32
    return pl.pallas_call(
        kernel,
        out_shape=jax.ShapeDtypeStruct((BLOCKS * BS, DSHARE), bf16),
        in_specs=[smem] * 3 + [hbm] * 4,
        out_specs=pl.BlockSpec(memory_space=pltpu.VMEM),
        scratch_shapes=[
            pltpu.VMEM((SEQ * 2, BS, KVW), bf16),
            pltpu.VMEM(out_weight.shape, bf16),
            pltpu.VMEM(queries.shape, bf16),
            pltpu.VMEM((BLOCKS * UNITS, HEAD_DIM, ROWS), f32),
            pltpu.VMEM((BLOCKS * UNITS, 8, ROWS), f32),
            pltpu.VMEM((BS, HEADS * HEAD_DIM), bf16),
            pltpu.VMEM((2, BS, HALF), f32),
            pltpu.VMEM((BLOCKS * BS, DSHARE), f32),
            pltpu.VMEM((BLOCKS, 6, BS, HALF), bf16),
            pltpu.VMEM((BLOCKS, 6, BS, HALF), bf16),
            pltpu.VMEM((BLOCKS, BS, KVW), bf16),
            pltpu.VMEM((BLOCKS, BS, KVW), bf16),
            pltpu.VMEM((BLOCKS, BS, KVW), bf16),
            pltpu.VMEM((BLOCKS, BS, KVW), bf16),
            pltpu.VMEM((4, 2, 4, BS, KVW), bf16),
            pltpu.VMEM((2, 4, BS, KVW), bf16),
            pltpu.VMEM((SEQ, BS, KVW), bf16),
            pltpu.VMEM((SIDE, 2, 8, 128), jnp.int32),
            pltpu.SMEM((SIDE, 2, 8, 128), jnp.int32),
            pltpu.SemaphoreType.DMA((5,)),
            pltpu.SemaphoreType.DMA((36,)),
            pltpu.SemaphoreType.DMA((36,)),
            pltpu.SemaphoreType.DMA((6,)),
            pltpu.SemaphoreType.DMA((6,)),
            pltpu.SemaphoreType.DMA((2, 4)),
            pltpu.SemaphoreType.DMA((2, 4)),
            pltpu.SemaphoreType.DMA((2, 4, 4)),
            pltpu.SemaphoreType.DMA((2, 4, 4)),
            pltpu.SemaphoreType.DMA((SIDE, 2)),
            pltpu.SemaphoreType.DMA((SIDE, 2)),
            pltpu.SemaphoreType.DMA((BLOCKS, 6)),
            pltpu.SemaphoreType.DMA((BLOCKS, 6)),
        ],
        compiler_params=pltpu.CompilerParams(
            collective_id=0, has_side_effects=True, vmem_limit_bytes=62 * 1024 * 1024
        ),
        name="tree_attention",
    )(image_of, ancestors, counts, queries, kv, im, out_weight)


def solution(mesh):
    in_specs = (
        P("seq", "head"),
        P("seq", None, "head"),
        P("seq", None, "head"),
        P("seq"),
        P("seq", None),
        P("seq"),
        P("head", None),
    )
    out_specs = P("seq", "head")
    return jax.shard_map(body, mesh=mesh, in_specs=in_specs, out_specs=out_specs, check_vma=False)
```

```python
import math

import jax
import jax.numpy as jnp
from jax import lax
from jax.experimental import pallas as pl
from jax.experimental.pallas import tpu as pltpu
from jax.sharding import PartitionSpec as P

HEAD_DIM = 128
BS = 128
IMG_TOK = 1024
ANC = 8
SIDE = 4
BLOCKS = 4
SEQ = 32
KVW = 512
HEADS = 16
GROUP = 4
UNITS = HEADS // GROUP
ROWS = GROUP * BS
DSHARE = 1024
HALF = 512
BIG = 1e30
SCALE2 = HEAD_DIM ** (-0.5) * math.log2(math.e)
MESH = pl.DeviceIdType.MESH
A_STEPS = (0, -1, 1, 2)
HALVES = (2, 3, 6, 7, 10, 11, 14, 15, 18, 19)


def kernel(
    image_of, ancestors, counts, q_in, kv_in, im_in, w_in, out_ref,
    kv_raw, im_raw, result, im, w, q, acc, stat, att, hold, own, stage, zrecv,
    row_own, row_prev, row_next, row_far, picked, passing, got, table, needs,
    local_sem, out_sem, im_send, im_recv, row_send, row_recv, pass_send, pass_recv, got_send, got_recv,
    table_send, table_recv, z_send, z_recv,
):
    me = lax.axis_index("seq")
    z = lax.axis_index("head")
    core = lax.rem(me, 2)
    x = lax.rem(me // 2, SIDE)
    y = me // (2 * SIDE)

    def chip(da, db, c):
        ox = lax.rem(x + da * (1 - c) + db * c + SIDE, SIDE)
        oy = lax.rem(y + da * c + db * (1 - c) + SIDE, SIDE)
        return (oy * SIDE + ox) * 2 + c

    def other(device):
        return device + 1 - 2 * core

    a_up, a_down = (chip(1, 0, core), z), (chip(-1, 0, core), z)
    b_up, b_down = (chip(0, 1, core), z), (chip(0, -1, core), z)
    sibling = (other(me), z)
    z_up, z_down = (me, lax.rem(z + 1, SIDE)), (me, lax.rem(z + SIDE - 1, SIDE))
    near = [sibling, z_up, z_down]
    for da, db in ((1, 0), (-1, 0), (2, 0), (0, 1), (0, -1), (0, 2)):
        near += [(chip(da, db, 0), z), (chip(da, db, 1), z)]

    locals_ = [
        pltpu.make_async_copy(kv_in, kv_raw, local_sem.at[0]),
        pltpu.make_async_copy(im_in, im_raw, local_sem.at[1]),
        pltpu.make_async_copy(q_in, q, local_sem.at[2]),
        pltpu.make_async_copy(w_in, w, local_sem.at[3]),
    ]
    for copy in locals_:
        copy.start()

    barrier = pltpu.get_barrier_semaphore()
    for device in near:
        pl.semaphore_signal(barrier, inc=1, device_id=device, device_id_type=MESH)

    lane = lax.broadcasted_iota(jnp.int32, (8, 128), 1)
    listed = jnp.zeros((8, 128), jnp.int32)
    for b in range(BLOCKS):
        for a in range(ANC):
            block = jnp.full((8, 128), ancestors[b, a], jnp.int32)
            listed = jnp.maximum(listed, jnp.where((block >> 2) == lane, block & 3, 0))
    table[0, 0] = listed

    to_row = lax.broadcasted_iota(jnp.int32, (2 * BS, 2 * BS), 0)
    from_row = lax.broadcasted_iota(jnp.int32, (2 * BS, 2 * BS), 1)
    wanted = jnp.where(to_row < BS, 2 * to_row, 2 * to_row - (2 * BS - 1))
    parting = jnp.where(from_row == wanted, 1.0, 0.0).astype(jnp.bfloat16)
    for raw, buf, first, count, copy in (
        (im_raw, im, me * 2, 2, locals_[1]), (kv_raw, row_own, 0, BLOCKS, locals_[0]),
    ):
        copy.wait()
        for n in range(count):
            turns = raw[n * BS : (n + 1) * BS].reshape(2 * BS, KVW // 2)
            parted = jnp.dot(parting, turns, preferred_element_type=jnp.float32).astype(jnp.bfloat16)
            buf[first + n, :, : KVW // 2] = parted[:BS]
            buf[first + n, :, KVW // 2 :] = parted[BS:]

    pl.semaphore_wait(barrier, len(near))

    def copy_to(src, dst, send, recv, device):
        return pltpu.make_async_remote_copy(
            src_ref=src, dst_ref=dst, send_sem=send, recv_sem=recv, device_id=device, device_id_type=MESH,
        )

    def wait_for(ref, sem):
        pltpu.make_async_copy(ref, ref, sem).wait()

    table_slots = [(k, r) for k in range(SIDE) for r in range(2) if (k, r) != (0, 0)]
    for k, r in table_slots:
        device = (chip(0, -k, core if r == 0 else 1 - core), z)
        copy_to(table.at[0, 0], table.at[k, r], table_send.at[k, r], table_recv.at[k, r], device).start()

    class Gather:
        def __init__(self, buf, source, n, send, recv):
            self.buf, self.source, self.n, self.send, self.recv = buf, source, n, send, recv
            self.started = []
            self.siblings = 0

        def rows(self, da, db, part=None, c=None):
            origin = chip(da, db, core if c is None else c)
            if part is None:
                return self.buf.at[pl.ds(origin * self.n, self.n)]
            half = self.n // 2
            return self.buf.at[pl.ds(origin * self.n + part * half, half)]

        def push(self, src, dst, device, index):
            pltpu.make_async_remote_copy(
                src_ref=src, dst_ref=dst, send_sem=self.send.at[index], recv_sem=self.recv.at[index],
                device_id=device, device_id_type=MESH,
            ).start()
            self.started.append(index)

        def arrive(self, ref, index):
            pltpu.make_async_copy(ref, ref, self.recv.at[index]).wait()

        def spread(self, da, src=None):
            ref = self.rows(da, 0)
            src = ref if src is None else src
            i = 4 + A_STEPS.index(da) * 4
            self.push(src, ref, b_up, i)
            self.push(src, ref, b_down, i + 1)

        def pair(self, da, db, src=None):
            ref = self.rows(da, db)
            self.push(ref if src is None else src, ref, sibling, 20 + self.siblings)
            self.siblings += 1

        def begin(self):
            ref = self.rows(0, 0)
            self.push(self.source, ref, a_up, 0)
            self.push(self.source, ref, a_down, 1)
            self.spread(0, self.source)
            self.pair(0, 0, self.source)

        def along_a(self):
            self.arrive(self.rows(-1, 0), 0)
            half = self.rows(-1, 0, 0)
            self.push(half, half, a_up, 2)
            self.spread(-1)
            self.pair(-1, 0)
            self.arrive(self.rows(1, 0), 1)
            half = self.rows(1, 0, 1)
            self.push(half, half, a_down, 3)
            self.spread(1)
            self.pair(1, 0)

        def far_a(self):
            self.arrive(self.rows(2, 0, 0), 2)
            self.arrive(self.rows(2, 0, 1), 3)
            self.spread(2)
            self.pair(2, 0)

        def along_b(self, da):
            i = 4 + A_STEPS.index(da) * 4
            self.arrive(self.rows(da, -1), i)
            half = self.rows(da, -1, 0)
            self.push(half, half, b_up, i + 2)
            self.pair(da, -1)
            self.arrive(self.rows(da, 1), i + 1)
            half = self.rows(da, 1, 1)
            self.push(half, half, b_down, i + 3)
            self.pair(da, 1)

        def far_b(self, da):
            i = 4 + A_STEPS.index(da) * 4
            self.arrive(self.rows(da, 2, 0), i + 2)
            self.arrive(self.rows(da, 2, 1), i + 3)
            self.pair(da, 2)

        def finish(self):
            order = [(0, 0), (-1, 0), (1, 0), (0, -1), (0, 1), (2, 0)]
            for da in A_STEPS[1:]:
                order += [(da, -1), (da, 1)]
            order += [(da, 2) for da in A_STEPS]
            for k, (da, db) in enumerate(order):
                self.arrive(self.rows(da, db, c=1 - core), 20 + k)

        def drain(self):
            for index in self.started:
                part = self.n // 2 if index in HALVES else self.n
                ref = self.buf.at[pl.ds(0, part)]
                pltpu.make_async_copy(ref, ref, self.send.at[index]).wait()

    images = Gather(im, im.at[pl.ds(me * 2, 2)], 2, im_send, im_recv)
    low, high = pl.ds(0, 2), pl.ds(2, 2)
    row_copies = [
        copy_to(row_own.at[low], row_prev.at[low], row_send.at[0], row_recv.at[0], a_up),
        copy_to(row_own.at[high], row_next.at[high], row_send.at[1], row_recv.at[1], a_down),
        copy_to(row_own.at[high], row_prev.at[high], row_send.at[2], row_recv.at[2], a_up),
        copy_to(row_own.at[low], row_next.at[low], row_send.at[3], row_recv.at[3], a_down),
        copy_to(row_prev.at[low], row_far.at[low], row_send.at[4], row_recv.at[4], a_up),
        copy_to(row_next.at[high], row_far.at[high], row_send.at[5], row_recv.at[5], a_down),
    ]

    def row_begin():
        for copy in row_copies[:4]:
            copy.start()

    def row_pass():
        row_copies[0].wait_recv()
        row_copies[4].start()
        row_copies[1].wait_recv()
        row_copies[5].start()

    SIDES = (0, -1, 1, 2)

    def origin(r, k, i):
        return chip(A_STEPS[i], SIDES[k], core if r == 0 else 1 - core)

    def deliver(src, r, k, i, source, device):
        if r == 1:
            device = (other(device[0]), z)
        return copy_to(src, got.at[source], got_send.at[r, k, i], got_recv.at[r, k, i], device)

    def pass_copy(r, i):
        device = b_up if i < 2 else b_down
        return copy_to(picked.at[2, r, i], passing.at[r, i], pass_send.at[r, i], pass_recv.at[r, i], device)

    def hand_on(r, i):
        device, back = (b_up, -1) if i < 2 else (b_down, 1)
        return deliver(passing.at[r, i], r, 3, i, chip(A_STEPS[i], back, core), device)

    def pick(i, row):
        source = chip(A_STEPS[i], 0, core)
        for r in range(2):
            picked[2, r, i] = row[needs[2, r, 0, source]]
            pass_copy(r, i).start()
        for n, (k, slot, device) in enumerate(((1, 1, b_up), (2, 3, b_down))):
            for r in range(2):
                picked[n, r, i] = row[needs[slot, r, 0, source]]
                deliver(picked.at[n, r, i], r, k, i, source, device).start()
        picked[3, 1, i] = row[needs[0, 1, 0, source]]
        deliver(picked.at[3, 1, i], 1, 0, i, source, (me, z)).start()
        got[source] = row[needs[0, 0, 0, source]]

    images.begin()
    row_copies[0].start()
    row_copies[1].start()
    images.along_a()
    for k, r in table_slots:
        wait_for(table.at[k, r], table_recv.at[k, r])
    to_scalars = pltpu.make_async_copy(table, needs, local_sem.at[4])
    to_scalars.start()
    images.along_b(0)
    images.far_a()
    row_copies[2].start()
    row_copies[3].start()
    to_scalars.wait()
    for da in A_STEPS[1:]:
        images.along_b(da)
    pick(0, row_own)
    for da in A_STEPS:
        images.far_b(da)
    row_pass()
    locals_[2].wait()
    images.finish()

    nt = (((1,), (1,)), ((), ()))
    nn = (((1,), (0,)), ((), ()))

    def dot(a, b, dims):
        return lax.dot_general(a, b, dims, preferred_element_type=jnp.float32)

    def queries_of(b, u):
        rows = pl.ds(pl.multiple_of(b * BS, BS), BS)
        lanes = [
            pl.ds(pl.multiple_of((u * GROUP + h) * HEAD_DIM, HEAD_DIM), HEAD_DIM) for h in range(GROUP)
        ]
        return jnp.concatenate([q[rows, cols] for cols in lanes], axis=0)

    def lanes_of(j):
        return (
            pl.ds(pl.multiple_of(j * HEAD_DIM, HEAD_DIM), HEAD_DIM),
            pl.ds(pl.multiple_of(256 + j * HEAD_DIM, HEAD_DIM), HEAD_DIM),
        )

    key_at = lax.broadcasted_iota(jnp.int32, (BS, ROWS), 0)
    token_at = lax.broadcasted_iota(jnp.int32, (BS, ROWS), 1) & (BS - 1)

    def image_part(b, j):
        lanes = lanes_of(j)
        image = image_of[b]
        k, v = (
            jnp.concatenate(
                [im[image * 8 + t, :, cols] for t in range(IMG_TOK // BS)] + [row_own[b, :, cols]], axis=0
            )
            for cols in lanes
        )
        v = v.T
        for r in range(2):
            u = 2 * j + r
            slot = b * UNITS + u
            s = dot(k, queries_of(b, u), nt)
            s, s_own = s[:IMG_TOK], s[IMG_TOK:]
            s_own = jnp.where(key_at <= token_at, s_own, -BIG)
            top = jnp.maximum(jnp.max(s, axis=0, keepdims=True), jnp.max(s_own, axis=0, keepdims=True))
            e = jnp.exp2((s - top) * SCALE2)
            e_own = jnp.exp2((s_own - top) * SCALE2)
            stat[slot, 0:1] = top
            stat[slot, 1:2] = jnp.sum(e, axis=0, keepdims=True) + jnp.sum(e_own, axis=0, keepdims=True)
            acc[slot] = dot(v, jnp.concatenate([e.astype(jnp.bfloat16), e_own.astype(jnp.bfloat16)], axis=0), nn)

    def rest_part(b, j):
        k_lanes, v_lanes = lanes_of(j)
        live = jnp.full((1, ROWS), counts[b], jnp.int32)
        at = [lax.shift_right_logical(ancestors[b, a], 2) for a in range(ANC)]
        k = jnp.concatenate([got[i, :, k_lanes] for i in at], axis=0)
        v = jnp.concatenate([got[i, :, v_lanes] for i in at], axis=0).T
        for r in range(2):
            u = 2 * j + r
            slot = b * UNITS + u
            s = dot(k, queries_of(b, u), nt)
            parts = [s[a * BS : (a + 1) * BS] for a in range(ANC)]
            before = stat[slot, 0:1]
            top = before
            for a in range(ANC):
                best = jnp.max(parts[a], axis=0, keepdims=True)
                top = jnp.maximum(top, jnp.where(live > a, best, -BIG))
            keep = jnp.exp2((before - top) * SCALE2)
            total = stat[slot, 1:2] * keep
            weights = []
            for a in range(ANC):
                under = jnp.where(live > a, top, BIG)
                e = jnp.exp2((parts[a] - under) * SCALE2)
                total = total + jnp.sum(e, axis=0, keepdims=True)
                weights.append(e.astype(jnp.bfloat16))
            o = acc[slot] * keep + dot(v, jnp.concatenate(weights, axis=0), nn)
            o = o / total
            for h in range(GROUP):
                cols = pl.ds(pl.multiple_of((u * GROUP + h) * HEAD_DIM, HEAD_DIM), HEAD_DIM)
                att[:, cols] = o[:, h * BS : (h + 1) * BS].T.astype(jnp.bfloat16)

    def project(d, half):
        cols = pl.ds(pl.multiple_of(d * DSHARE + half * HALF, HALF), HALF)
        return dot(att[...], w[:, cols], nn)

    far, up, down = lax.rem(z + 2, SIDE), lax.rem(z + 1, SIDE), lax.rem(z + 3, SIDE)

    def z_copy(b, slot, device):
        return pltpu.make_async_remote_copy(
            src_ref=stage.at[b, slot], dst_ref=zrecv.at[b, slot],
            send_sem=z_send.at[b, slot], recv_sem=z_recv.at[b, slot],
            device_id=device, device_id_type=MESH,
        )

    def z_wait(b, slot):
        wait_for(zrecv.at[b, slot], z_recv.at[b, slot])

    def pass_on(b):
        for k, (slot, device) in enumerate(((4, z_up), (5, z_down))):
            z_wait(b, k)
            stage[b, slot] = (hold[k] + zrecv[b, k].astype(jnp.float32)).astype(jnp.bfloat16)
            z_copy(b, slot, device).start()

    def one_block(b, carry):
        def heads(j, carry):
            rest_part(b, j)
            return carry

        lax.fori_loop(0, 2, heads, 0)

        def send_partial(slot, d, half, device):
            stage[b, slot] = project(d, half).astype(jnp.bfloat16)
            z_copy(b, slot, device).start()

        send_partial(0, far, 0, z_up)
        send_partial(1, far, 1, z_down)
        pl.when(b > 0)(lambda: pass_on(b - 1))
        send_partial(2, up, 1, z_up)
        send_partial(3, down, 0, z_down)
        hold[0] = project(up, 0)
        hold[1] = project(down, 1)
        for half in range(2):
            own[pl.ds(pl.multiple_of(b * BS, BS), BS), half * HALF : (half + 1) * HALF] = project(z, half)
        return carry

    def forward(i):
        for r in range(2):
            pass_copy(r, i).wait_recv()
            hand_on(r, i).start()

    def image_step(i, carry):
        def mid_pick():
            row_copies[2].wait_recv()
            pick(1, row_prev)
            row_copies[3].wait_recv()
            pick(2, row_next)

        def last_pick():
            row_copies[4].wait_recv()
            row_copies[5].wait_recv()
            pick(3, row_far)

        pl.when(i == 0)(mid_pick)
        pl.when(i == 1)(last_pick)
        for step, n in ((2, 0), (2, 1), (3, 2), (4, 3)):
            pl.when(i == step)(lambda n=n: forward(n))
        image_part(i // 2, lax.rem(i, 2))
        return carry

    lax.fori_loop(0, 2 * BLOCKS, image_step, 0)
    arrivals = [(r, k, i) for r in range(2) for k in range(4) for i in range(4) if (r, k) != (0, 0)]
    for r, k, i in arrivals:
        wait_for(got.at[origin(r, k, i)], got_recv.at[r, k, i])
    locals_[3].wait()
    lax.fori_loop(0, BLOCKS, one_block, 0)
    pass_on(BLOCKS - 1)

    def out_copy(b):
        rows = pl.ds(pl.multiple_of(b * BS, BS), BS)
        return pltpu.make_async_copy(result.at[rows], out_ref.at[rows], out_sem.at[b])

    def last(b, carry):
        rows = pl.ds(pl.multiple_of(b * BS, BS), BS)
        for slot in (2, 3, 4, 5):
            z_wait(b, slot)
        for half, (one, two) in enumerate(((3, 4), (2, 5))):
            cols = slice(half * HALF, (half + 1) * HALF)
            total = own[rows, cols] + zrecv[b, one].astype(jnp.float32) + zrecv[b, two].astype(jnp.float32)
            result[rows, cols] = total.astype(jnp.bfloat16)
        out_copy(b).start()
        for slot in range(6):
            wait_for(stage.at[b, slot], z_send.at[b, slot])
        return carry

    lax.fori_loop(0, BLOCKS, last, 0)
    images.drain()
    for b in range(BLOCKS):
        out_copy(b).wait()
    for k, r in table_slots:
        wait_for(table.at[0, 0], table_send.at[k, r])
    for copy in row_copies:
        copy.wait_send()
    for r in range(2):
        for i in range(4):
            pass_copy(r, i).wait_send()
    for r, k, i in arrivals:
        wait_for(got.at[0], got_send.at[r, k, i])


def body(queries, keys_values, image_kv, image_of, ancestors, counts, out_weight):
    smem = pl.BlockSpec(memory_space=pltpu.SMEM)
    hbm = pl.BlockSpec(memory_space=pl.ANY)
    bf16, f32 = jnp.bfloat16, jnp.float32
    return pl.pallas_call(
        kernel,
        out_shape=jax.ShapeDtypeStruct((BLOCKS * BS, DSHARE), bf16),
        in_specs=[smem] * 3 + [hbm] * 4,
        out_specs=hbm,
        scratch_shapes=[
            pltpu.VMEM(keys_values.shape, bf16),
            pltpu.VMEM(image_kv.shape, bf16),
            pltpu.VMEM((BLOCKS * BS, DSHARE), bf16),
            pltpu.VMEM((SEQ * 2, BS, KVW), bf16),
            pltpu.VMEM(out_weight.shape, bf16),
            pltpu.VMEM(queries.shape, bf16),
            pltpu.VMEM((BLOCKS * UNITS, HEAD_DIM, ROWS), f32),
            pltpu.VMEM((BLOCKS * UNITS, 8, ROWS), f32),
            pltpu.VMEM((BS, HEADS * HEAD_DIM), bf16),
            pltpu.VMEM((2, BS, HALF), f32),
            pltpu.VMEM((BLOCKS * BS, DSHARE), f32),
            pltpu.VMEM((BLOCKS, 6, BS, HALF), bf16),
            pltpu.VMEM((BLOCKS, 6, BS, HALF), bf16),
            pltpu.VMEM((BLOCKS, BS, KVW), bf16),
            pltpu.VMEM((BLOCKS, BS, KVW), bf16),
            pltpu.VMEM((BLOCKS, BS, KVW), bf16),
            pltpu.VMEM((BLOCKS, BS, KVW), bf16),
            pltpu.VMEM((4, 2, 4, BS, KVW), bf16),
            pltpu.VMEM((2, 4, BS, KVW), bf16),
            pltpu.VMEM((SEQ, BS, KVW), bf16),
            pltpu.VMEM((SIDE, 2, 8, 128), jnp.int32),
            pltpu.SMEM((SIDE, 2, 8, 128), jnp.int32),
            pltpu.SemaphoreType.DMA((5,)),
            pltpu.SemaphoreType.DMA((BLOCKS,)),
            pltpu.SemaphoreType.DMA((36,)),
            pltpu.SemaphoreType.DMA((36,)),
            pltpu.SemaphoreType.DMA((6,)),
            pltpu.SemaphoreType.DMA((6,)),
            pltpu.SemaphoreType.DMA((2, 4)),
            pltpu.SemaphoreType.DMA((2, 4)),
            pltpu.SemaphoreType.DMA((2, 4, 4)),
            pltpu.SemaphoreType.DMA((2, 4, 4)),
            pltpu.SemaphoreType.DMA((SIDE, 2)),
            pltpu.SemaphoreType.DMA((SIDE, 2)),
            pltpu.SemaphoreType.DMA((BLOCKS, 6)),
            pltpu.SemaphoreType.DMA((BLOCKS, 6)),
        ],
        compiler_params=pltpu.CompilerParams(
            collective_id=0, has_side_effects=True, vmem_limit_bytes=62 * 1024 * 1024
        ),
        name="tree_attention",
    )(image_of, ancestors, counts, queries, keys_values, image_kv, out_weight)


def solution(mesh):
    in_specs = (
        P("seq", "head"),
        P("seq", None, "head"),
        P("seq", None, "head"),
        P("seq"),
        P("seq", None),
        P("seq"),
        P("head", None),
    )
    out_specs = P("seq", "head")
    return jax.shard_map(body, mesh=mesh, in_specs=in_specs, out_specs=out_specs, check_vma=False)
```

```python
import math

import jax
import jax.numpy as jnp
from jax import lax
from jax.experimental import pallas as pl
from jax.experimental.pallas import tpu as pltpu
from jax.sharding import PartitionSpec as P

HEAD_DIM = 128
BS = 128
IMG_TOK = 1024
ANC = 8
SIDE = 4
BLOCKS = 4
SEQ = 32
KVW = 512
HEADS = 16
GROUP = 8
KV_HEADS = HEADS // GROUP
ROWS = GROUP * BS
DSHARE = 1024
HALF = 512
BIG = 1e30
SCALE2 = HEAD_DIM ** (-0.5) * math.log2(math.e)
MESH = pl.DeviceIdType.MESH
A_STEPS = (0, -1, 1, 2)
HALVES = (2, 3, 6, 7, 10, 11, 14, 15, 18, 19)


def kernel(
    image_of, ancestors, counts, q_in, kv_in, im_in, w_in, out_ref,
    kv_raw, im_raw, result, im, w, q, acc, stat, att, hold, own, stage, zrecv,
    row_own, row_prev, row_next, row_far, picked, passing, got, table, needs,
    local_sem, out_sem, im_send, im_recv, row_send, row_recv, pass_send, pass_recv, got_send, got_recv,
    table_send, table_recv, z_send, z_recv,
):
    me = lax.axis_index("seq")
    z = lax.axis_index("head")
    core = lax.rem(me, 2)
    x = lax.rem(me // 2, SIDE)
    y = me // (2 * SIDE)

    def chip(da, db, c):
        ox = lax.rem(x + da * (1 - c) + db * c + SIDE, SIDE)
        oy = lax.rem(y + da * c + db * (1 - c) + SIDE, SIDE)
        return (oy * SIDE + ox) * 2 + c

    def other(device):
        return device + 1 - 2 * core

    a_up, a_down = (chip(1, 0, core), z), (chip(-1, 0, core), z)
    b_up, b_down = (chip(0, 1, core), z), (chip(0, -1, core), z)
    sibling = (other(me), z)
    z_up, z_down = (me, lax.rem(z + 1, SIDE)), (me, lax.rem(z + SIDE - 1, SIDE))
    near = [sibling, z_up, z_down]
    for da, db in ((1, 0), (-1, 0), (2, 0), (0, 1), (0, -1), (0, 2)):
        near += [(chip(da, db, 0), z), (chip(da, db, 1), z)]

    locals_ = [
        pltpu.make_async_copy(kv_in, kv_raw, local_sem.at[0]),
        pltpu.make_async_copy(im_in, im_raw, local_sem.at[1]),
        pltpu.make_async_copy(q_in, q, local_sem.at[2]),
        pltpu.make_async_copy(w_in, w, local_sem.at[3]),
    ]
    for copy in locals_:
        copy.start()

    barrier = pltpu.get_barrier_semaphore()
    for device in near:
        pl.semaphore_signal(barrier, inc=1, device_id=device, device_id_type=MESH)

    lane = lax.broadcasted_iota(jnp.int32, (8, 128), 1)
    listed = jnp.zeros((8, 128), jnp.int32)
    for b in range(BLOCKS):
        for a in range(ANC):
            block = jnp.full((8, 128), ancestors[b, a], jnp.int32)
            listed = jnp.maximum(listed, jnp.where((block >> 2) == lane, block & 3, 0))
    table[0, 0] = listed

    to_row = lax.broadcasted_iota(jnp.int32, (2 * BS, 2 * BS), 0)
    from_row = lax.broadcasted_iota(jnp.int32, (2 * BS, 2 * BS), 1)
    wanted = jnp.where(to_row < BS, 2 * to_row, 2 * to_row - (2 * BS - 1))
    parting = jnp.where(from_row == wanted, 1.0, 0.0).astype(jnp.bfloat16)
    for raw, buf, first, count, copy in (
        (im_raw, im, me * 2, 2, locals_[1]), (kv_raw, row_own, 0, BLOCKS, locals_[0]),
    ):
        copy.wait()
        for n in range(count):
            turns = raw[n * BS : (n + 1) * BS].reshape(2 * BS, KVW // 2)
            parted = jnp.dot(parting, turns, preferred_element_type=jnp.float32).astype(jnp.bfloat16)
            buf[first + n, :, : KVW // 2] = parted[:BS]
            buf[first + n, :, KVW // 2 :] = parted[BS:]

    pl.semaphore_wait(barrier, len(near))

    def copy_to(src, dst, send, recv, device):
        return pltpu.make_async_remote_copy(
            src_ref=src, dst_ref=dst, send_sem=send, recv_sem=recv, device_id=device, device_id_type=MESH,
        )

    def wait_for(ref, sem):
        pltpu.make_async_copy(ref, ref, sem).wait()

    table_slots = [(k, r) for k in range(SIDE) for r in range(2) if (k, r) != (0, 0)]
    for k, r in table_slots:
        device = (chip(0, -k, core if r == 0 else 1 - core), z)
        copy_to(table.at[0, 0], table.at[k, r], table_send.at[k, r], table_recv.at[k, r], device).start()

    class Gather:
        def __init__(self, buf, source, n, send, recv):
            self.buf, self.source, self.n, self.send, self.recv = buf, source, n, send, recv
            self.started = []
            self.siblings = 0

        def rows(self, da, db, part=None, c=None):
            origin = chip(da, db, core if c is None else c)
            if part is None:
                return self.buf.at[pl.ds(origin * self.n, self.n)]
            half = self.n // 2
            return self.buf.at[pl.ds(origin * self.n + part * half, half)]

        def push(self, src, dst, device, index):
            pltpu.make_async_remote_copy(
                src_ref=src, dst_ref=dst, send_sem=self.send.at[index], recv_sem=self.recv.at[index],
                device_id=device, device_id_type=MESH,
            ).start()
            self.started.append(index)

        def arrive(self, ref, index):
            pltpu.make_async_copy(ref, ref, self.recv.at[index]).wait()

        def spread(self, da, src=None):
            ref = self.rows(da, 0)
            src = ref if src is None else src
            i = 4 + A_STEPS.index(da) * 4
            self.push(src, ref, b_up, i)
            self.push(src, ref, b_down, i + 1)

        def pair(self, da, db, src=None):
            ref = self.rows(da, db)
            self.push(ref if src is None else src, ref, sibling, 20 + self.siblings)
            self.siblings += 1

        def begin(self):
            ref = self.rows(0, 0)
            self.push(self.source, ref, a_up, 0)
            self.push(self.source, ref, a_down, 1)
            self.spread(0, self.source)
            self.pair(0, 0, self.source)

        def along_a(self):
            self.arrive(self.rows(-1, 0), 0)
            half = self.rows(-1, 0, 0)
            self.push(half, half, a_up, 2)
            self.spread(-1)
            self.pair(-1, 0)
            self.arrive(self.rows(1, 0), 1)
            half = self.rows(1, 0, 1)
            self.push(half, half, a_down, 3)
            self.spread(1)
            self.pair(1, 0)

        def far_a(self):
            self.arrive(self.rows(2, 0, 0), 2)
            self.arrive(self.rows(2, 0, 1), 3)
            self.spread(2)
            self.pair(2, 0)

        def along_b(self, da):
            i = 4 + A_STEPS.index(da) * 4
            self.arrive(self.rows(da, -1), i)
            half = self.rows(da, -1, 0)
            self.push(half, half, b_up, i + 2)
            self.pair(da, -1)
            self.arrive(self.rows(da, 1), i + 1)
            half = self.rows(da, 1, 1)
            self.push(half, half, b_down, i + 3)
            self.pair(da, 1)

        def far_b(self, da):
            i = 4 + A_STEPS.index(da) * 4
            self.arrive(self.rows(da, 2, 0), i + 2)
            self.arrive(self.rows(da, 2, 1), i + 3)
            self.pair(da, 2)

        def finish(self):
            order = [(0, 0), (-1, 0), (1, 0), (0, -1), (0, 1), (2, 0)]
            for da in A_STEPS[1:]:
                order += [(da, -1), (da, 1)]
            order += [(da, 2) for da in A_STEPS]
            for k, (da, db) in enumerate(order):
                self.arrive(self.rows(da, db, c=1 - core), 20 + k)

        def drain(self):
            for index in self.started:
                part = self.n // 2 if index in HALVES else self.n
                ref = self.buf.at[pl.ds(0, part)]
                pltpu.make_async_copy(ref, ref, self.send.at[index]).wait()

    images = Gather(im, im.at[pl.ds(me * 2, 2)], 2, im_send, im_recv)
    low, high = pl.ds(0, 2), pl.ds(2, 2)
    row_copies = [
        copy_to(row_own.at[low], row_prev.at[low], row_send.at[0], row_recv.at[0], a_up),
        copy_to(row_own.at[high], row_next.at[high], row_send.at[1], row_recv.at[1], a_down),
        copy_to(row_own.at[high], row_prev.at[high], row_send.at[2], row_recv.at[2], a_up),
        copy_to(row_own.at[low], row_next.at[low], row_send.at[3], row_recv.at[3], a_down),
        copy_to(row_prev.at[low], row_far.at[low], row_send.at[4], row_recv.at[4], a_up),
        copy_to(row_next.at[high], row_far.at[high], row_send.at[5], row_recv.at[5], a_down),
    ]

    def row_begin():
        for copy in row_copies[:4]:
            copy.start()

    def row_pass():
        row_copies[0].wait_recv()
        row_copies[4].start()
        row_copies[1].wait_recv()
        row_copies[5].start()

    SIDES = (0, -1, 1, 2)

    def origin(r, k, i):
        return chip(A_STEPS[i], SIDES[k], core if r == 0 else 1 - core)

    def deliver(src, r, k, i, source, device):
        if r == 1:
            device = (other(device[0]), z)
        return copy_to(src, got.at[source], got_send.at[r, k, i], got_recv.at[r, k, i], device)

    def pass_copy(r, i):
        device = b_up if i < 2 else b_down
        return copy_to(picked.at[2, r, i], passing.at[r, i], pass_send.at[r, i], pass_recv.at[r, i], device)

    def hand_on(r, i):
        device, back = (b_up, -1) if i < 2 else (b_down, 1)
        return deliver(passing.at[r, i], r, 3, i, chip(A_STEPS[i], back, core), device)

    def pick(i, row):
        source = chip(A_STEPS[i], 0, core)
        for r in range(2):
            picked[2, r, i] = row[needs[2, r, 0, source]]
            pass_copy(r, i).start()
        for n, (k, slot, device) in enumerate(((1, 1, b_up), (2, 3, b_down))):
            for r in range(2):
                picked[n, r, i] = row[needs[slot, r, 0, source]]
                deliver(picked.at[n, r, i], r, k, i, source, device).start()
        picked[3, 1, i] = row[needs[0, 1, 0, source]]
        deliver(picked.at[3, 1, i], 1, 0, i, source, (me, z)).start()
        got[source] = row[needs[0, 0, 0, source]]

    images.begin()
    row_copies[0].start()
    row_copies[1].start()
    images.along_a()
    for k, r in table_slots:
        wait_for(table.at[k, r], table_recv.at[k, r])
    to_scalars = pltpu.make_async_copy(table, needs, local_sem.at[4])
    to_scalars.start()
    images.along_b(0)
    images.far_a()
    row_copies[2].start()
    row_copies[3].start()
    to_scalars.wait()
    for da in A_STEPS[1:]:
        images.along_b(da)
    pick(0, row_own)
    for da in A_STEPS:
        images.far_b(da)
    row_pass()
    locals_[2].wait()
    images.finish()

    nt = (((1,), (1,)), ((), ()))
    nn = (((1,), (0,)), ((), ()))

    def dot(a, b, dims):
        return lax.dot_general(a, b, dims, preferred_element_type=jnp.float32)

    def queries_of(b, u):
        rows = pl.ds(pl.multiple_of(b * BS, BS), BS)
        lanes = [
            pl.ds(pl.multiple_of((u * GROUP + h) * HEAD_DIM, HEAD_DIM), HEAD_DIM) for h in range(GROUP)
        ]
        return jnp.concatenate([q[rows, cols] for cols in lanes], axis=0)

    def heads_of(blocks, j):
        k = jnp.concatenate([ref[i, :, j * HEAD_DIM : (j + 1) * HEAD_DIM] for ref, i in blocks], axis=0)
        at = 256 + j * HEAD_DIM
        v = jnp.concatenate([ref[i, :, at : at + HEAD_DIM] for ref, i in blocks], axis=0)
        return k, jnp.concatenate([v.T, jnp.ones((16, v.shape[0]), jnp.bfloat16)], axis=0)

    key_at = lax.broadcasted_iota(jnp.int32, (BS, ROWS), 0)
    token_at = lax.broadcasted_iota(jnp.int32, (BS, ROWS), 1) & (BS - 1)

    def image_part(b):
        image = image_of[b]
        blocks = [(im, image * 8 + t) for t in range(IMG_TOK // BS)] + [(row_own, b)]
        heads = [heads_of(blocks, j) for j in range(KV_HEADS)]
        scores = [dot(heads[j][0], queries_of(b, j), nt) for j in range(KV_HEADS)]
        for j in range(KV_HEADS):
            slot = b * KV_HEADS + j
            s, s_own = scores[j][:IMG_TOK], scores[j][IMG_TOK:]
            s_own = jnp.where(key_at <= token_at, s_own, -BIG)
            top = jnp.maximum(jnp.max(s, axis=0, keepdims=True), jnp.max(s_own, axis=0, keepdims=True))
            e = jnp.exp2((s - top) * SCALE2).astype(jnp.bfloat16)
            e_own = jnp.exp2((s_own - top) * SCALE2).astype(jnp.bfloat16)
            o = dot(heads[j][1], jnp.concatenate([e, e_own], axis=0), nn)
            stat[slot, 0:1] = top
            stat[slot, 1:2] = o[HEAD_DIM : HEAD_DIM + 1]
            acc[slot] = o[:HEAD_DIM]

    def rest_part(b):
        live = jnp.full((1, ROWS), counts[b], jnp.int32)
        blocks = [(got, lax.shift_right_logical(ancestors[b, a], 2)) for a in range(ANC)]
        heads = [heads_of(blocks, j) for j in range(KV_HEADS)]
        scores = [dot(heads[j][0], queries_of(b, j), nt) for j in range(KV_HEADS)]
        for j in range(KV_HEADS):
            slot = b * KV_HEADS + j
            parts = [scores[j][a * BS : (a + 1) * BS] for a in range(ANC)]
            before = stat[slot, 0:1]
            top = before
            for a in range(ANC):
                best = jnp.max(parts[a], axis=0, keepdims=True)
                top = jnp.maximum(top, jnp.where(live > a, best, -BIG))
            keep = jnp.exp2((before - top) * SCALE2)
            weights = []
            for a in range(ANC):
                under = jnp.where(live > a, top, BIG)
                weights.append(jnp.exp2((parts[a] - under) * SCALE2).astype(jnp.bfloat16))
            o = dot(heads[j][1], jnp.concatenate(weights, axis=0), nn)
            total = stat[slot, 1:2] * keep + o[HEAD_DIM : HEAD_DIM + 1]
            o = (acc[slot] * keep + o[:HEAD_DIM]) / total
            for h in range(GROUP):
                at = (j * GROUP + h) * HEAD_DIM
                att[:, at : at + HEAD_DIM] = o[:, h * BS : (h + 1) * BS].T.astype(jnp.bfloat16)

    def project(d, half):
        cols = pl.ds(pl.multiple_of(d * DSHARE + half * HALF, HALF), HALF)
        return dot(att[...], w[:, cols], nn)

    far, up, down = lax.rem(z + 2, SIDE), lax.rem(z + 1, SIDE), lax.rem(z + 3, SIDE)

    def z_copy(b, slot, device):
        return pltpu.make_async_remote_copy(
            src_ref=stage.at[b, slot], dst_ref=zrecv.at[b, slot],
            send_sem=z_send.at[b, slot], recv_sem=z_recv.at[b, slot],
            device_id=device, device_id_type=MESH,
        )

    def z_wait(b, slot):
        wait_for(zrecv.at[b, slot], z_recv.at[b, slot])

    def pass_on(b):
        for k, (slot, device) in enumerate(((4, z_up), (5, z_down))):
            z_wait(b, k)
            stage[b, slot] = (hold[k] + zrecv[b, k].astype(jnp.float32)).astype(jnp.bfloat16)
            z_copy(b, slot, device).start()

    def one_block(b, carry):
        rest_part(b)

        def send_partial(slot, d, half, device):
            stage[b, slot] = project(d, half).astype(jnp.bfloat16)
            z_copy(b, slot, device).start()

        send_partial(0, far, 0, z_up)
        send_partial(1, far, 1, z_down)
        pl.when(b > 0)(lambda: pass_on(b - 1))
        send_partial(2, up, 1, z_up)
        send_partial(3, down, 0, z_down)
        hold[0] = project(up, 0)
        hold[1] = project(down, 1)
        for half in range(2):
            own[pl.ds(pl.multiple_of(b * BS, BS), BS), half * HALF : (half + 1) * HALF] = project(z, half)
        return carry

    def forward(i):
        for r in range(2):
            pass_copy(r, i).wait_recv()
            hand_on(r, i).start()

    def image_step(i, carry):
        def mid_pick():
            row_copies[2].wait_recv()
            pick(1, row_prev)
            row_copies[3].wait_recv()
            pick(2, row_next)

        def last_pick():
            row_copies[4].wait_recv()
            row_copies[5].wait_recv()
            pick(3, row_far)

        pl.when(i == 0)(mid_pick)
        pl.when(i == 1)(last_pick)
        for step, n in ((1, 0), (1, 1), (2, 2), (3, 3)):
            pl.when(i == step)(lambda n=n: forward(n))
        image_part(i)
        return carry

    lax.fori_loop(0, BLOCKS, image_step, 0)
    arrivals = [(r, k, i) for r in range(2) for k in range(4) for i in range(4) if (r, k) != (0, 0)]
    for r, k, i in arrivals:
        wait_for(got.at[origin(r, k, i)], got_recv.at[r, k, i])
    locals_[3].wait()
    lax.fori_loop(0, BLOCKS, one_block, 0)
    pass_on(BLOCKS - 1)

    def out_copy(b):
        rows = pl.ds(pl.multiple_of(b * BS, BS), BS)
        return pltpu.make_async_copy(result.at[rows], out_ref.at[rows], out_sem.at[b])

    def last(b, carry):
        rows = pl.ds(pl.multiple_of(b * BS, BS), BS)
        for slot in (2, 3, 4, 5):
            z_wait(b, slot)
        for half, (one, two) in enumerate(((3, 4), (2, 5))):
            cols = slice(half * HALF, (half + 1) * HALF)
            total = own[rows, cols] + zrecv[b, one].astype(jnp.float32) + zrecv[b, two].astype(jnp.float32)
            result[rows, cols] = total.astype(jnp.bfloat16)
        out_copy(b).start()
        for slot in range(6):
            wait_for(stage.at[b, slot], z_send.at[b, slot])
        return carry

    lax.fori_loop(0, BLOCKS, last, 0)
    images.drain()
    for b in range(BLOCKS):
        out_copy(b).wait()
    for k, r in table_slots:
        wait_for(table.at[0, 0], table_send.at[k, r])
    for copy in row_copies:
        copy.wait_send()
    for r in range(2):
        for i in range(4):
            pass_copy(r, i).wait_send()
    for r, k, i in arrivals:
        wait_for(got.at[0], got_send.at[r, k, i])


def body(queries, keys_values, image_kv, image_of, ancestors, counts, out_weight):
    smem = pl.BlockSpec(memory_space=pltpu.SMEM)
    hbm = pl.BlockSpec(memory_space=pl.ANY)
    bf16, f32 = jnp.bfloat16, jnp.float32
    return pl.pallas_call(
        kernel,
        out_shape=jax.ShapeDtypeStruct((BLOCKS * BS, DSHARE), bf16),
        in_specs=[smem] * 3 + [hbm] * 4,
        out_specs=hbm,
        scratch_shapes=[
            pltpu.VMEM(keys_values.shape, bf16),
            pltpu.VMEM(image_kv.shape, bf16),
            pltpu.VMEM((BLOCKS * BS, DSHARE), bf16),
            pltpu.VMEM((SEQ * 2, BS, KVW), bf16),
            pltpu.VMEM(out_weight.shape, bf16),
            pltpu.VMEM(queries.shape, bf16),
            pltpu.VMEM((BLOCKS * KV_HEADS, HEAD_DIM, ROWS), f32),
            pltpu.VMEM((BLOCKS * KV_HEADS, 8, ROWS), f32),
            pltpu.VMEM((BS, HEADS * HEAD_DIM), bf16),
            pltpu.VMEM((2, BS, HALF), f32),
            pltpu.VMEM((BLOCKS * BS, DSHARE), f32),
            pltpu.VMEM((BLOCKS, 6, BS, HALF), bf16),
            pltpu.VMEM((BLOCKS, 6, BS, HALF), bf16),
            pltpu.VMEM((BLOCKS, BS, KVW), bf16),
            pltpu.VMEM((BLOCKS, BS, KVW), bf16),
            pltpu.VMEM((BLOCKS, BS, KVW), bf16),
            pltpu.VMEM((BLOCKS, BS, KVW), bf16),
            pltpu.VMEM((4, 2, 4, BS, KVW), bf16),
            pltpu.VMEM((2, 4, BS, KVW), bf16),
            pltpu.VMEM((SEQ, BS, KVW), bf16),
            pltpu.VMEM((SIDE, 2, 8, 128), jnp.int32),
            pltpu.SMEM((SIDE, 2, 8, 128), jnp.int32),
            pltpu.SemaphoreType.DMA((5,)),
            pltpu.SemaphoreType.DMA((BLOCKS,)),
            pltpu.SemaphoreType.DMA((36,)),
            pltpu.SemaphoreType.DMA((36,)),
            pltpu.SemaphoreType.DMA((6,)),
            pltpu.SemaphoreType.DMA((6,)),
            pltpu.SemaphoreType.DMA((2, 4)),
            pltpu.SemaphoreType.DMA((2, 4)),
            pltpu.SemaphoreType.DMA((2, 4, 4)),
            pltpu.SemaphoreType.DMA((2, 4, 4)),
            pltpu.SemaphoreType.DMA((SIDE, 2)),
            pltpu.SemaphoreType.DMA((SIDE, 2)),
            pltpu.SemaphoreType.DMA((BLOCKS, 6)),
            pltpu.SemaphoreType.DMA((BLOCKS, 6)),
        ],
        compiler_params=pltpu.CompilerParams(
            collective_id=0, has_side_effects=True, vmem_limit_bytes=62 * 1024 * 1024
        ),
        name="tree_attention",
    )(image_of, ancestors, counts, queries, keys_values, image_kv, out_weight)


def solution(mesh):
    in_specs = (
        P("seq", "head"),
        P("seq", None, "head"),
        P("seq", None, "head"),
        P("seq"),
        P("seq", None),
        P("seq"),
        P("head", None),
    )
    out_specs = P("seq", "head")
    return jax.shard_map(body, mesh=mesh, in_specs=in_specs, out_specs=out_specs, check_vma=False)
```

```python
import math

import jax
import jax.numpy as jnp
from jax import lax
from jax.experimental import pallas as pl
from jax.experimental.pallas import tpu as pltpu
from jax.sharding import PartitionSpec as P

HEAD_DIM = 128
BS = 128
IMG_TOK = 1024
ANC = 8
SIDE = 4
BLOCKS = 4
SEQ = 32
KVW = 512
HEADS = 16
GROUP = 8
KV_HEADS = HEADS // GROUP
ROWS = GROUP * BS
DSHARE = 1024
HALF = 512
BIG = 1e30
SCALE2 = HEAD_DIM ** (-0.5) * math.log2(math.e)
MESH = pl.DeviceIdType.MESH
A_STEPS = (0, -1, 1, 2)
HALVES = (2, 3, 6, 7, 10, 11, 14, 15, 18, 19)


def kernel(
    image_of, ancestors, counts, q_in, kv_in, im_in, w_in, out_ref,
    kv_raw, im_raw, result, im, w, q, acc, stat, att, hold, own, stage, zrecv,
    row_own, row_prev, row_next, row_far, picked, passing, got, table, needs,
    local_sem, out_sem, im_send, im_recv, row_send, row_recv, pass_send, pass_recv, got_send, got_recv,
    table_send, table_recv, z_send, z_recv,
):
    me = lax.axis_index("seq")
    z = lax.axis_index("head")
    core = lax.rem(me, 2)
    x = lax.rem(me // 2, SIDE)
    y = me // (2 * SIDE)

    def chip(da, db, c):
        ox = lax.rem(x + da * (1 - c) + db * c + SIDE, SIDE)
        oy = lax.rem(y + da * c + db * (1 - c) + SIDE, SIDE)
        return (oy * SIDE + ox) * 2 + c

    def other(device):
        return device + 1 - 2 * core

    a_up, a_down = (chip(1, 0, core), z), (chip(-1, 0, core), z)
    b_up, b_down = (chip(0, 1, core), z), (chip(0, -1, core), z)
    sibling = (other(me), z)
    z_up, z_down = (me, lax.rem(z + 1, SIDE)), (me, lax.rem(z + SIDE - 1, SIDE))
    near = [sibling, z_up, z_down]
    for da, db in ((1, 0), (-1, 0), (2, 0), (0, 1), (0, -1), (0, 2)):
        near += [(chip(da, db, 0), z), (chip(da, db, 1), z)]

    locals_ = [
        pltpu.make_async_copy(kv_in, kv_raw, local_sem.at[0]),
        pltpu.make_async_copy(im_in, im_raw, local_sem.at[1]),
        pltpu.make_async_copy(q_in, q, local_sem.at[2]),
        pltpu.make_async_copy(w_in, w, local_sem.at[3]),
    ]
    for copy in locals_:
        copy.start()

    barrier = pltpu.get_barrier_semaphore()
    for device in near:
        pl.semaphore_signal(barrier, inc=1, device_id=device, device_id_type=MESH)

    lane = lax.broadcasted_iota(jnp.int32, (8, 128), 1)
    listed = jnp.zeros((8, 128), jnp.int32)
    for b in range(BLOCKS):
        for a in range(ANC):
            block = jnp.full((8, 128), ancestors[b, a], jnp.int32)
            listed = jnp.maximum(listed, jnp.where((block >> 2) == lane, block & 3, 0))
    table[0, 0] = listed

    to_row = lax.broadcasted_iota(jnp.int32, (2 * BS, 2 * BS), 0)
    from_row = lax.broadcasted_iota(jnp.int32, (2 * BS, 2 * BS), 1)
    wanted = jnp.where(to_row < BS, 2 * to_row, 2 * to_row - (2 * BS - 1))
    parting = jnp.where(from_row == wanted, 1.0, 0.0).astype(jnp.bfloat16)
    for raw, buf, first, count, copy in (
        (im_raw, im, me * 2, 2, locals_[1]), (kv_raw, row_own, 0, BLOCKS, locals_[0]),
    ):
        copy.wait()
        for n in range(count):
            turns = raw[n * BS : (n + 1) * BS].reshape(2 * BS, KVW // 2)
            parted = jnp.dot(parting, turns, preferred_element_type=jnp.float32).astype(jnp.bfloat16)
            buf[first + n, :, : KVW // 2] = parted[:BS]
            buf[first + n, :, KVW // 2 :] = parted[BS:]

    pl.semaphore_wait(barrier, len(near))

    def copy_to(src, dst, send, recv, device):
        return pltpu.make_async_remote_copy(
            src_ref=src, dst_ref=dst, send_sem=send, recv_sem=recv, device_id=device, device_id_type=MESH,
        )

    def wait_for(ref, sem):
        pltpu.make_async_copy(ref, ref, sem).wait()

    table_slots = [(k, r) for k in range(SIDE) for r in range(2) if (k, r) != (0, 0)]
    for k, r in table_slots:
        device = (chip(0, -k, core if r == 0 else 1 - core), z)
        copy_to(table.at[0, 0], table.at[k, r], table_send.at[k, r], table_recv.at[k, r], device).start()

    class Gather:
        def __init__(self, buf, source, n, send, recv):
            self.buf, self.source, self.n, self.send, self.recv = buf, source, n, send, recv
            self.started = []
            self.siblings = 0

        def rows(self, da, db, part=None, c=None):
            origin = chip(da, db, core if c is None else c)
            if part is None:
                return self.buf.at[pl.ds(origin * self.n, self.n)]
            half = self.n // 2
            return self.buf.at[pl.ds(origin * self.n + part * half, half)]

        def push(self, src, dst, device, index):
            pltpu.make_async_remote_copy(
                src_ref=src, dst_ref=dst, send_sem=self.send.at[index], recv_sem=self.recv.at[index],
                device_id=device, device_id_type=MESH,
            ).start()
            self.started.append(index)

        def arrive(self, ref, index):
            pltpu.make_async_copy(ref, ref, self.recv.at[index]).wait()

        def spread(self, da, src=None):
            ref = self.rows(da, 0)
            src = ref if src is None else src
            i = 4 + A_STEPS.index(da) * 4
            self.push(src, ref, b_up, i)
            self.push(src, ref, b_down, i + 1)

        def pair(self, da, db, src=None):
            ref = self.rows(da, db)
            self.push(ref if src is None else src, ref, sibling, 20 + self.siblings)
            self.siblings += 1

        def begin(self):
            ref = self.rows(0, 0)
            self.push(self.source, ref, a_up, 0)
            self.push(self.source, ref, a_down, 1)
            self.spread(0, self.source)
            self.pair(0, 0, self.source)

        def along_a(self):
            self.arrive(self.rows(-1, 0), 0)
            half = self.rows(-1, 0, 0)
            self.push(half, half, a_up, 2)
            self.spread(-1)
            self.pair(-1, 0)
            self.arrive(self.rows(1, 0), 1)
            half = self.rows(1, 0, 1)
            self.push(half, half, a_down, 3)
            self.spread(1)
            self.pair(1, 0)

        def far_a(self):
            self.arrive(self.rows(2, 0, 0), 2)
            self.arrive(self.rows(2, 0, 1), 3)
            self.spread(2)
            self.pair(2, 0)

        def along_b(self, da):
            i = 4 + A_STEPS.index(da) * 4
            self.arrive(self.rows(da, -1), i)
            half = self.rows(da, -1, 0)
            self.push(half, half, b_up, i + 2)
            self.pair(da, -1)
            self.arrive(self.rows(da, 1), i + 1)
            half = self.rows(da, 1, 1)
            self.push(half, half, b_down, i + 3)
            self.pair(da, 1)

        def far_b(self, da):
            i = 4 + A_STEPS.index(da) * 4
            self.arrive(self.rows(da, 2, 0), i + 2)
            self.arrive(self.rows(da, 2, 1), i + 3)
            self.pair(da, 2)

        def finish(self):
            order = [(0, 0), (-1, 0), (1, 0), (0, -1), (0, 1), (2, 0)]
            for da in A_STEPS[1:]:
                order += [(da, -1), (da, 1)]
            order += [(da, 2) for da in A_STEPS]
            for k, (da, db) in enumerate(order):
                self.arrive(self.rows(da, db, c=1 - core), 20 + k)

        def drain(self):
            for index in self.started:
                part = self.n // 2 if index in HALVES else self.n
                ref = self.buf.at[pl.ds(0, part)]
                pltpu.make_async_copy(ref, ref, self.send.at[index]).wait()

    images = Gather(im, im.at[pl.ds(me * 2, 2)], 2, im_send, im_recv)
    low, high = pl.ds(0, 2), pl.ds(2, 2)
    row_copies = [
        copy_to(row_own.at[low], row_prev.at[low], row_send.at[0], row_recv.at[0], a_up),
        copy_to(row_own.at[high], row_next.at[high], row_send.at[1], row_recv.at[1], a_down),
        copy_to(row_own.at[high], row_prev.at[high], row_send.at[2], row_recv.at[2], a_up),
        copy_to(row_own.at[low], row_next.at[low], row_send.at[3], row_recv.at[3], a_down),
        copy_to(row_prev.at[low], row_far.at[low], row_send.at[4], row_recv.at[4], a_up),
        copy_to(row_next.at[high], row_far.at[high], row_send.at[5], row_recv.at[5], a_down),
    ]

    def row_begin():
        for copy in row_copies[:4]:
            copy.start()

    def row_pass():
        row_copies[0].wait_recv()
        row_copies[4].start()
        row_copies[1].wait_recv()
        row_copies[5].start()

    SIDES = (0, -1, 1, 2)

    def origin(r, k, i):
        return chip(A_STEPS[i], SIDES[k], core if r == 0 else 1 - core)

    def deliver(src, r, k, i, source, device):
        if r == 1:
            device = (other(device[0]), z)
        return copy_to(src, got.at[source], got_send.at[r, k, i], got_recv.at[r, k, i], device)

    def pass_copy(r, i):
        device = b_up if i < 2 else b_down
        return copy_to(picked.at[2, r, i], passing.at[r, i], pass_send.at[r, i], pass_recv.at[r, i], device)

    def hand_on(r, i):
        device, back = (b_up, -1) if i < 2 else (b_down, 1)
        return deliver(passing.at[r, i], r, 3, i, chip(A_STEPS[i], back, core), device)

    def pick(i, row):
        source = chip(A_STEPS[i], 0, core)
        for r in range(2):
            picked[2, r, i] = row[needs[2, r, 0, source]]
            pass_copy(r, i).start()
        for n, (k, slot, device) in enumerate(((1, 1, b_up), (2, 3, b_down))):
            for r in range(2):
                picked[n, r, i] = row[needs[slot, r, 0, source]]
                deliver(picked.at[n, r, i], r, k, i, source, device).start()
        picked[3, 1, i] = row[needs[0, 1, 0, source]]
        deliver(picked.at[3, 1, i], 1, 0, i, source, (me, z)).start()
        got[source] = row[needs[0, 0, 0, source]]

    images.begin()
    row_copies[0].start()
    row_copies[1].start()
    images.along_a()
    for k, r in table_slots:
        wait_for(table.at[k, r], table_recv.at[k, r])
    to_scalars = pltpu.make_async_copy(table, needs, local_sem.at[4])
    to_scalars.start()
    images.along_b(0)
    images.far_a()
    row_copies[2].start()
    row_copies[3].start()
    to_scalars.wait()
    for da in A_STEPS[1:]:
        images.along_b(da)
    pick(0, row_own)
    for da in A_STEPS:
        images.far_b(da)
    row_pass()
    locals_[2].wait()
    images.finish()

    nt = (((1,), (1,)), ((), ()))
    nn = (((1,), (0,)), ((), ()))

    def dot(a, b, dims):
        return lax.dot_general(a, b, dims, preferred_element_type=jnp.float32)

    def queries_of(b, u):
        rows = pl.ds(pl.multiple_of(b * BS, BS), BS)
        lanes = [
            pl.ds(pl.multiple_of((u * GROUP + h) * HEAD_DIM, HEAD_DIM), HEAD_DIM) for h in range(GROUP)
        ]
        return jnp.concatenate([q[rows, cols] for cols in lanes], axis=0)

    def heads_of(blocks, j):
        k = jnp.concatenate([ref[i, :, j * HEAD_DIM : (j + 1) * HEAD_DIM] for ref, i in blocks], axis=0)
        at = 256 + j * HEAD_DIM
        v = jnp.concatenate([ref[i, :, at : at + HEAD_DIM] for ref, i in blocks], axis=0)
        return k, jnp.concatenate([v.T, jnp.ones((16, v.shape[0]), jnp.bfloat16)], axis=0)

    key_at = lax.broadcasted_iota(jnp.int32, (BS, ROWS), 0)
    token_at = lax.broadcasted_iota(jnp.int32, (BS, ROWS), 1) & (BS - 1)

    def image_part(b):
        image = image_of[b]
        blocks = [(im, image * 8 + t) for t in range(IMG_TOK // BS)] + [(row_own, b)]
        heads = [heads_of(blocks, j) for j in range(KV_HEADS)]
        scores = [dot(heads[j][0], queries_of(b, j), nt) for j in range(KV_HEADS)]
        for j in range(KV_HEADS):
            slot = b * KV_HEADS + j
            s, s_own = scores[j][:IMG_TOK], scores[j][IMG_TOK:]
            s_own = jnp.where(key_at <= token_at, s_own, -BIG)
            top = jnp.maximum(jnp.max(s, axis=0, keepdims=True), jnp.max(s_own, axis=0, keepdims=True))
            e = jnp.exp2((s - top) * SCALE2).astype(jnp.bfloat16)
            e_own = jnp.exp2((s_own - top) * SCALE2).astype(jnp.bfloat16)
            o = dot(heads[j][1], jnp.concatenate([e, e_own], axis=0), nn)
            stat[slot, 0:1] = top
            stat[slot, 1:2] = o[HEAD_DIM : HEAD_DIM + 1]
            acc[slot] = o[:HEAD_DIM]

    def rest_part(b):
        live = jnp.full((1, ROWS), counts[b], jnp.int32)
        blocks = [(got, lax.shift_right_logical(ancestors[b, a], 2)) for a in range(ANC)]
        heads = [heads_of(blocks, j) for j in range(KV_HEADS)]
        scores = [dot(heads[j][0], queries_of(b, j), nt) for j in range(KV_HEADS)]
        for j in range(KV_HEADS):
            slot = b * KV_HEADS + j
            parts = [scores[j][a * BS : (a + 1) * BS] for a in range(ANC)]
            before = stat[slot, 0:1]
            top = before
            for a in range(ANC):
                best = jnp.max(parts[a], axis=0, keepdims=True)
                top = jnp.maximum(top, jnp.where(live > a, best, -BIG))
            keep = jnp.exp2((before - top) * SCALE2)
            weights = []
            for a in range(ANC):
                under = jnp.where(live > a, top, BIG)
                weights.append(jnp.exp2((parts[a] - under) * SCALE2).astype(jnp.bfloat16))
            o = dot(heads[j][1], jnp.concatenate(weights, axis=0), nn)
            total = stat[slot, 1:2] * keep + o[HEAD_DIM : HEAD_DIM + 1]
            o = (acc[slot] * keep + o[:HEAD_DIM]) / total
            for h in range(GROUP):
                at = (j * GROUP + h) * HEAD_DIM
                att[:, at : at + HEAD_DIM] = o[:, h * BS : (h + 1) * BS].T.astype(jnp.bfloat16)

    def project(d, half):
        cols = pl.ds(pl.multiple_of(d * DSHARE + half * HALF, HALF), HALF)
        return dot(att[...], w[:, cols], nn)

    far, up, down = lax.rem(z + 2, SIDE), lax.rem(z + 1, SIDE), lax.rem(z + 3, SIDE)

    def z_copy(b, slot, device):
        return pltpu.make_async_remote_copy(
            src_ref=stage.at[b, slot], dst_ref=zrecv.at[b, slot],
            send_sem=z_send.at[b, slot], recv_sem=z_recv.at[b, slot],
            device_id=device, device_id_type=MESH,
        )

    def z_wait(b, slot):
        wait_for(zrecv.at[b, slot], z_recv.at[b, slot])

    def pass_on(b):
        for k, (slot, device) in enumerate(((4, z_up), (5, z_down))):
            z_wait(b, k)
            stage[b, slot] = (hold[k] + zrecv[b, k].astype(jnp.float32)).astype(jnp.bfloat16)
            z_copy(b, slot, device).start()

    def one_block(b, carry):
        rest_part(b)

        def send_partial(slot, d, half, device):
            stage[b, slot] = project(d, half).astype(jnp.bfloat16)
            z_copy(b, slot, device).start()

        send_partial(0, far, 0, z_up)
        send_partial(1, far, 1, z_down)
        pl.when(b > 0)(lambda: pass_on(b - 1))
        send_partial(2, up, 1, z_up)
        send_partial(3, down, 0, z_down)
        hold[0] = project(up, 0)
        hold[1] = project(down, 1)
        for half in range(2):
            own[pl.ds(pl.multiple_of(b * BS, BS), BS), half * HALF : (half + 1) * HALF] = project(z, half)
        return carry

    def forward(i):
        for r in range(2):
            pass_copy(r, i).wait_recv()
            hand_on(r, i).start()

    def image_step(i, carry):
        def mid_pick():
            row_copies[2].wait_recv()
            pick(1, row_prev)
            row_copies[3].wait_recv()
            pick(2, row_next)

        def last_pick():
            row_copies[4].wait_recv()
            row_copies[5].wait_recv()
            pick(3, row_far)

        pl.when(i == 0)(mid_pick)
        pl.when(i == 1)(last_pick)
        for step, n in ((1, 0), (1, 1), (2, 2), (3, 3)):
            pl.when(i == step)(lambda n=n: forward(n))
        image_part(i)
        return carry

    lax.fori_loop(0, BLOCKS, image_step, 0)
    arrivals = [(r, k, i) for r in range(2) for k in range(4) for i in range(4) if (r, k) != (0, 0)]
    for r, k, i in arrivals:
        wait_for(got.at[origin(r, k, i)], got_recv.at[r, k, i])
    locals_[3].wait()
    lax.fori_loop(0, BLOCKS, one_block, 0)
    images.drain()
    for k, r in table_slots:
        wait_for(table.at[0, 0], table_send.at[k, r])
    for copy in row_copies:
        copy.wait_send()
    for r in range(2):
        for i in range(4):
            pass_copy(r, i).wait_send()
    for r, k, i in arrivals:
        wait_for(got.at[0], got_send.at[r, k, i])
    pass_on(BLOCKS - 1)

    def out_copy(b):
        rows = pl.ds(pl.multiple_of(b * BS, BS), BS)
        return pltpu.make_async_copy(result.at[rows], out_ref.at[rows], out_sem.at[b])

    def last(b, carry):
        rows = pl.ds(pl.multiple_of(b * BS, BS), BS)
        for slot in (2, 3, 4, 5):
            z_wait(b, slot)
        for half, (one, two) in enumerate(((3, 4), (2, 5))):
            cols = slice(half * HALF, (half + 1) * HALF)
            total = own[rows, cols] + zrecv[b, one].astype(jnp.float32) + zrecv[b, two].astype(jnp.float32)
            result[rows, cols] = total.astype(jnp.bfloat16)
        out_copy(b).start()
        return carry

    lax.fori_loop(0, BLOCKS, last, 0)
    for b in range(BLOCKS):
        for slot in range(6):
            wait_for(stage.at[b, slot], z_send.at[b, slot])
    for b in range(BLOCKS):
        out_copy(b).wait()


def body(queries, keys_values, image_kv, image_of, ancestors, counts, out_weight):
    smem = pl.BlockSpec(memory_space=pltpu.SMEM)
    hbm = pl.BlockSpec(memory_space=pl.ANY)
    bf16, f32 = jnp.bfloat16, jnp.float32
    return pl.pallas_call(
        kernel,
        out_shape=jax.ShapeDtypeStruct((BLOCKS * BS, DSHARE), bf16),
        in_specs=[smem] * 3 + [hbm] * 4,
        out_specs=hbm,
        scratch_shapes=[
            pltpu.VMEM(keys_values.shape, bf16),
            pltpu.VMEM(image_kv.shape, bf16),
            pltpu.VMEM((BLOCKS * BS, DSHARE), bf16),
            pltpu.VMEM((SEQ * 2, BS, KVW), bf16),
            pltpu.VMEM(out_weight.shape, bf16),
            pltpu.VMEM(queries.shape, bf16),
            pltpu.VMEM((BLOCKS * KV_HEADS, HEAD_DIM, ROWS), f32),
            pltpu.VMEM((BLOCKS * KV_HEADS, 8, ROWS), f32),
            pltpu.VMEM((BS, HEADS * HEAD_DIM), bf16),
            pltpu.VMEM((2, BS, HALF), f32),
            pltpu.VMEM((BLOCKS * BS, DSHARE), f32),
            pltpu.VMEM((BLOCKS, 6, BS, HALF), bf16),
            pltpu.VMEM((BLOCKS, 6, BS, HALF), bf16),
            pltpu.VMEM((BLOCKS, BS, KVW), bf16),
            pltpu.VMEM((BLOCKS, BS, KVW), bf16),
            pltpu.VMEM((BLOCKS, BS, KVW), bf16),
            pltpu.VMEM((BLOCKS, BS, KVW), bf16),
            pltpu.VMEM((4, 2, 4, BS, KVW), bf16),
            pltpu.VMEM((2, 4, BS, KVW), bf16),
            pltpu.VMEM((SEQ, BS, KVW), bf16),
            pltpu.VMEM((SIDE, 2, 8, 128), jnp.int32),
            pltpu.SMEM((SIDE, 2, 8, 128), jnp.int32),
            pltpu.SemaphoreType.DMA((5,)),
            pltpu.SemaphoreType.DMA((BLOCKS,)),
            pltpu.SemaphoreType.DMA((36,)),
            pltpu.SemaphoreType.DMA((36,)),
            pltpu.SemaphoreType.DMA((6,)),
            pltpu.SemaphoreType.DMA((6,)),
            pltpu.SemaphoreType.DMA((2, 4)),
            pltpu.SemaphoreType.DMA((2, 4)),
            pltpu.SemaphoreType.DMA((2, 4, 4)),
            pltpu.SemaphoreType.DMA((2, 4, 4)),
            pltpu.SemaphoreType.DMA((SIDE, 2)),
            pltpu.SemaphoreType.DMA((SIDE, 2)),
            pltpu.SemaphoreType.DMA((BLOCKS, 6)),
            pltpu.SemaphoreType.DMA((BLOCKS, 6)),
        ],
        compiler_params=pltpu.CompilerParams(
            collective_id=0, has_side_effects=True, vmem_limit_bytes=62 * 1024 * 1024
        ),
        name="tree_attention",
    )(image_of, ancestors, counts, queries, keys_values, image_kv, out_weight)


def solution(mesh):
    in_specs = (
        P("seq", "head"),
        P("seq", None, "head"),
        P("seq", None, "head"),
        P("seq"),
        P("seq", None),
        P("seq"),
        P("head", None),
    )
    out_specs = P("seq", "head")
    return jax.shard_map(body, mesh=mesh, in_specs=in_specs, out_specs=out_specs, check_vma=False)
```
